256 devices in a mesh: seq: 32 (over z, x), tp: 8 (over y, core).
Axes of the slice: x: 4, y: 4, z: 8, core: 2. Of those that a mesh axis runs over, the one named last changes fastest.
Arguments:
- hidden_new: bfloat16 [3, 16, 8192], P(None, None, 'seq'), may hold values from -6 to 6
- w_kv: bfloat16 [8192, 8, 256], P('seq', 'tp'), may hold values from -0.0625 to 0.0625
- w_out: bfloat16 [8192, 8192], P('tp', 'seq'), may hold values from -0.0625 to 0.0625
- queries_draft: bfloat16 [3, 4, 8, 32, 128], P(None, None, 'tp'), may hold values from -48 to 48
- queries_verify: bfloat16 [3, 4, 8, 32, 128], P(None, None, 'tp'), may hold values from -48 to 48
- keys_cache: bfloat16 [4, 8, 65536, 128], P(None, 'tp', 'seq'), may hold values from -6 to 6
- values_cache: bfloat16 [4, 8, 65536, 128], P(None, 'tp', 'seq'), may hold values from -6 to 6
- key_levels: bfloat16 [4, 8, 65536, 128], P(None, 'tp', 'seq'), may hold values from -8 to 7, as said below
- value_levels: bfloat16 [4, 8, 65536, 128], P(None, 'tp', 'seq'), may hold values from -8 to 7, as said below
- key_scales: float32 [4, 8, 65536], P(None, 'tp', 'seq'), may hold values from 0.05 to 0.5
- value_scales: float32 [4, 8, 65536], P(None, 'tp', 'seq'), may hold values from 0.1 to 0.4
- lengths: int32 [4], replicated, may hold values from 2 to 65528, as said below
- accepted: int32 [2, 4], replicated, may hold values from 0 to 4, as said below
Outputs:
- layer_out: bfloat16 [3, 2, 16, 8192], P(None, None, None, 'seq')
The draws below stay inside these ranges and needn't reach their ends.
Inputs may be any that keep to these rules, and one draw needn't show every extreme that they name: `key_levels`: every entry is a whole number. Positions 0 and 1 of every sequence and head hold equal levels. `value_levels`: every entry is a whole number. `lengths`: some sequence starts with exactly 65528 valid positions, another with 16 or fewer. `accepted`: the values 0 and 4 both occur.
All inputs are finite; a program needn't handle non-finite values.
Results may differ from the reference program's by a relative error of at most 0.006.
The reference program's roundings to bfloat16 on the way count: a program that leaves them out, or rounds other values in their place, can miss the bound.
Values may be sent and summed in bfloat16 or wider, within the bound.
No kernel may reach another device: no remote copies, remote signals or barrier semaphores. Data moves between devices by JAX's collectives and lax.ppermute only.
A program may use at most 128 MiB of HBM per device.

```python
import math
import jax
import jax.numpy as jnp
from jax import lax

D = 8192
KVH = 8
HD = 128
GROUP = 8
B = 4
S_DEV = 2048
R = 4
ROUNDS = 3
CTX = 65536
N_SEQ = 32


def first_levels(key):
    return jax.random.randint(jax.random.fold_in(key, 902), (B, KVH, HD), -8, 8, dtype=jnp.int32).astype(jnp.float32)


def broad_rows(key, label, base_rows):
    shape_full = (ROUNDS, B, KVH, GROUP * R, HD)
    chosen = jax.random.randint(jax.random.fold_in(key, label), (ROUNDS, B, KVH, GROUP * R), 0, 8) == 0
    signs = jnp.where(jax.random.bernoulli(jax.random.fold_in(key, label + 1), 0.5, shape_full), 1.0, -1.0)
    magnitude = jax.random.uniform(jax.random.fold_in(key, label + 2), shape_full, jnp.float32, 24.0, 48.0)
    return jnp.where(chosen[..., None], signs * magnitude, base_rows)


def draw_queries_draft(key, part):
    base_rows = jnp.clip(3.0 * jax.random.normal(jax.random.fold_in(key, 31), (ROUNDS, B, KVH, GROUP * R, HD), jnp.float32), -12.0, 12.0)
    base_rows = broad_rows(key, 71, base_rows)
    return base_rows.astype(jnp.bfloat16)


def draw_queries_verify(key, part):
    base_rows = jnp.clip(3.0 * jax.random.normal(jax.random.fold_in(key, 32), (ROUNDS, B, KVH, GROUP * R, HD), jnp.float32), -12.0, 12.0)
    base_rows = broad_rows(key, 81, base_rows)
    return base_rows.astype(jnp.bfloat16)


def draw_keys_cache(key, part):
    base_rows = jnp.clip(jax.random.normal(jax.random.fold_in(key, 33), (B, KVH, CTX, HD), jnp.float32), -6.0, 6.0)
    return base_rows.astype(jnp.bfloat16)


def draw_key_scales(key, part):
    uniform_log = jax.random.uniform(jax.random.fold_in(key, 34), (B, KVH, CTX), jnp.float32)
    scales = jnp.exp(math.log(0.15) + uniform_log * (math.log(0.3) - math.log(0.15)))
    return scales


def draw_key_levels(key, part):
    levels = jax.random.randint(jax.random.fold_in(key, 61), (B, KVH, CTX, HD), -8, 8, dtype=jnp.int32).astype(jnp.float32)
    leading = first_levels(key)
    levels = levels.at[:, :, 0, :].set(leading).at[:, :, 1, :].set(leading)
    return levels.astype(jnp.bfloat16)


def draw_value_levels(key, part):
    levels = jax.random.randint(jax.random.fold_in(key, 62), (B, KVH, CTX, HD), -8, 8, dtype=jnp.int32).astype(jnp.float32)
    return levels.astype(jnp.bfloat16)


def draw_lengths(key, part):
    longest = CTX - (ROUNDS - 1) * R
    top_bits = max(longest.bit_length() - 1, 1)
    exponents = jax.random.randint(jax.random.fold_in(key, 51), (B,), 1, top_bits + 1, dtype=jnp.int32)
    lowest = jnp.left_shift(jnp.ones((B,), jnp.int32), exponents)
    values_drawn = jax.random.randint(jax.random.fold_in(key, 52), (B,), lowest, 2 * lowest, dtype=jnp.int32)
    values_drawn = jnp.clip(values_drawn, 2, longest)
    picked = jax.random.randint(jax.random.fold_in(key, 55), (), 0, B, dtype=jnp.int32)
    other = (picked + jax.random.randint(jax.random.fold_in(key, 56), (), 1, B, dtype=jnp.int32)) % B
    short_len = jax.random.randint(jax.random.fold_in(key, 57), (), 2, min(17, longest + 1), dtype=jnp.int32)
    return values_drawn.at[picked].set(longest).at[other].set(short_len).astype(jnp.int32)


def draw_accepted(key, part):
    counts = jax.random.randint(jax.random.fold_in(key, 53), ((ROUNDS - 1) * B,), 0, R + 1, dtype=jnp.int32)
    picked = jax.random.permutation(jax.random.fold_in(key, 54), (ROUNDS - 1) * B)
    counts = counts.at[picked[0]].set(R).at[picked[1]].set(0)
    return counts.reshape(ROUNDS - 1, B).astype(jnp.int32)


def block_scale(rng, shape, pieces, least, top_value):
    loudness = 1.0
    for dim, blocks in pieces:
        steps = jax.random.uniform(jax.random.fold_in(jax.random.fold_in(rng, 6), dim), (blocks,), jnp.float32, least / len(pieces), top_value / len(pieces))
        loudness = loudness * jnp.repeat(jnp.exp(steps), shape[dim] // blocks).reshape((-1,) + (1,) * (len(shape) - 1 - dim))
    return loudness


def scatter_about(stream_key, shape, width, limit, split=(), held_as=jnp.bfloat16):
    result = jax.random.normal(stream_key, shape, jnp.float32) * width
    if len(split) > 0:
        result = block_scale(stream_key, shape, split, -0.22, 0.18) * result
    return jnp.clip(result, min=-limit, max=limit).astype(held_as)


def setup_inputs(seed: int = 0) -> dict:
    arg_keys = jax.random.split(jax.random.key(seed), 14)
    return {
        "hidden_new": scatter_about(arg_keys[0], (ROUNDS, B * R, D), 1.0, 6.0, ((2, 32),)),
        "w_kv": scatter_about(arg_keys[1], (D, KVH, 2 * HD), D ** -0.5, 0.0625, ((0, 32), (1, 8))),
        "w_out": scatter_about(arg_keys[2], (KVH * GROUP * HD, D), (KVH * GROUP * HD) ** -0.5, 0.0625, ((0, 8), (1, 32))),
        "queries_draft": draw_queries_draft(jax.random.fold_in(arg_keys[13], 71), 0),
        "queries_verify": draw_queries_verify(jax.random.fold_in(arg_keys[13], 71), 0),
        "keys_cache": draw_keys_cache(jax.random.fold_in(arg_keys[13], 71), 0),
        "values_cache": scatter_about(arg_keys[6], (B, KVH, CTX, HD), 1.0, 6.0, ((1, 8), (2, 32))),
        "key_levels": draw_key_levels(jax.random.fold_in(arg_keys[13], 71), 0),
        "value_levels": draw_value_levels(jax.random.fold_in(arg_keys[13], 71), 0),
        "key_scales": draw_key_scales(jax.random.fold_in(arg_keys[13], 71), 0),
        "value_scales": jnp.clip(jnp.exp(math.log(0.4) - 1.3862944 * jax.random.uniform(arg_keys[10], (B, KVH, CTX), jnp.float32) ** block_scale(arg_keys[10], (B, KVH, CTX), ((1, 8), (2, 32)), -0.2, 0.2)), 0.1, 0.4),
        "lengths": draw_lengths(jax.random.fold_in(arg_keys[13], 71), 0),
        "accepted": draw_accepted(jax.random.fold_in(arg_keys[13], 71), 0),
    }


NEG = -1e+30

def dequantize(levels, scales):
    return (levels.astype(jnp.float32) * scales[..., None]).astype(jnp.bfloat16)

def attend(queries, keys, values, usable):
    scores = jnp.einsum('bhqd,bhkd->bhqk', queries.astype(jnp.float32), keys.astype(jnp.float32)) * (1.0 / math.sqrt(HD))
    scores = jnp.where(usable, scores, NEG)
    maxima = lax.optimization_barrier(jnp.max(scores, axis=-1))
    weights = jnp.where(usable, jnp.exp(scores - maxima[..., None]), 0.0).astype(jnp.bfloat16)
    totals = lax.optimization_barrier(jnp.sum(weights.astype(jnp.float32), axis=-1))
    weighted = jnp.einsum('bhqk,bhkd->bhqd', weights.astype(jnp.float32), values.astype(jnp.float32))
    return (maxima, totals, weighted)

def combine(former, latter):
    highest = jnp.maximum(former[0], latter[0])
    former_w = jnp.exp(former[0] - highest)
    latter_w = jnp.exp(latter[0] - highest)
    return (highest, former[1] * former_w + latter[1] * latter_w, former[2] * former_w[..., None] + latter[2] * latter_w[..., None])

def finish(partial_value):
    return (partial_value[2] / partial_value[1][..., None]).astype(jnp.bfloat16)

def arrange(attended):
    return attended.reshape(2, B, KVH, GROUP, R, HD).transpose(0, 1, 4, 2, 3, 5).reshape(2 * B * R, KVH * GROUP * HD)

def reference(hidden_new, w_kv, w_out, queries_draft, queries_verify, keys_cache, values_cache, key_levels, value_levels, key_scales, value_scales, lengths, accepted):
    flat_kv = w_kv.reshape(D, KVH * 2 * HD)
    tokens = jnp.arange(GROUP * R, dtype=jnp.int32) % R
    causal = (tokens[:, None] >= jnp.arange(R, dtype=jnp.int32)[None, :])[None, None]
    offsets = jnp.arange(R, dtype=jnp.int32)[None, :]
    batch_rows = jnp.broadcast_to(jnp.arange(B, dtype=jnp.int32)[:, None], (B, R))
    blocks = jnp.arange(N_SEQ, dtype=jnp.int32)
    length_now = lengths
    results = []
    for turn_index in range(ROUNDS):
        fresh_rows = jnp.dot(hidden_new[turn_index], flat_kv, preferred_element_type=jnp.float32).astype(jnp.bfloat16).reshape(B, R, KVH, 2, HD)
        new_keys = fresh_rows[:, :, :, 0].transpose(0, 2, 1, 3)
        new_values = fresh_rows[:, :, :, 1].transpose(0, 2, 1, 3)
        draft_q = queries_draft[turn_index]
        verify_q = queries_verify[turn_index]

        def visit(running, block_index):
            first_row = block_index * S_DEV
            key_rows = lax.dynamic_slice_in_dim(keys_cache, first_row, S_DEV, 2)
            value_rows = lax.dynamic_slice_in_dim(values_cache, first_row, S_DEV, 2)
            key_low = dequantize(lax.dynamic_slice_in_dim(key_levels, first_row, S_DEV, 2), lax.dynamic_slice_in_dim(key_scales, first_row, S_DEV, 2))
            value_low = dequantize(lax.dynamic_slice_in_dim(value_levels, first_row, S_DEV, 2), lax.dynamic_slice_in_dim(value_scales, first_row, S_DEV, 2))
            places = first_row + jnp.arange(S_DEV, dtype=jnp.int32)
            stored = (places[None, :] < lengths[:, None])[:, None, :, None]
            usable = (places[None, :] < length_now[:, None])[:, None, None, :]
            draft_keys = jnp.where(stored, key_low, key_rows)
            draft_values = jnp.where(stored, value_low, value_rows)
            draft_part = attend(draft_q, draft_keys, draft_values, usable)
            verify_part = attend(verify_q, key_rows, value_rows, usable)
            return ((combine(running[0], draft_part), combine(running[1], verify_part)), None)
        initial = (jnp.full((B, KVH, GROUP * R), NEG, jnp.float32), jnp.zeros((B, KVH, GROUP * R), jnp.float32), jnp.zeros((B, KVH, GROUP * R, HD), jnp.float32))
        merged, unused = lax.scan(visit, (initial, initial), blocks)
        draft_all = combine(merged[0], attend(draft_q, new_keys, new_values, causal))
        verify_all = combine(merged[1], attend(verify_q, new_keys, new_values, causal))
        attended = jnp.stack([finish(draft_all), finish(verify_all)])
        projected = jnp.dot(arrange(attended), w_out, preferred_element_type=jnp.float32)
        results.append(projected.astype(jnp.bfloat16).reshape(2, B * R, D))
        if turn_index + 1 < ROUNDS:
            accepted_now = accepted[turn_index]
            places = jnp.where(offsets < accepted_now[:, None], length_now[:, None] + offsets, CTX)
            keys_cache = keys_cache.at[batch_rows, :, places, :].set(fresh_rows[:, :, :, 0], mode='drop')
            values_cache = values_cache.at[batch_rows, :, places, :].set(fresh_rows[:, :, :, 1], mode='drop')
            length_now = length_now + accepted_now
    return jnp.stack(results)
```

```python
import functools
import math

import jax
import jax.numpy as jnp
from jax import lax
from jax.experimental import pallas as pl
from jax.experimental.pallas import tpu as pltpu
from jax.sharding import PartitionSpec as P

HD = 128
GROUP = 8
R = 4
ROUNDS = 3
BATCH = 4
KINDS = 2
NEG = -1e30
SCALE = 1.0 / math.sqrt(HD)
SCALE_2 = SCALE / math.log(2.0)
ROWS = ROUNDS * GROUP * R
SHARE = KINDS * ROUNDS * R
NEW = ROUNDS * R
TOKENS = KINDS * ROUNDS * BATCH * R
AT_STATS = SHARE
AT_HIGH = SHARE + 8
AT_LOW = AT_HIGH + 2 * NEW
MESSAGE = AT_LOW + 2 * NEW
STEP = 512
VMEM_LIMIT = 48 * 1024 * 1024

f32 = jnp.float32
bf16 = jnp.bfloat16


def rounded(x):
    return x.astype(bf16).astype(f32)


def dot(a, b):
    return jnp.dot(a, b, preferred_element_type=f32)


def dot_rows(a, b):
    return lax.dot_general(a, b, (((1,), (1,)), ((), ())), preferred_element_type=f32)


def lanes_folded(x, op):
    folded = x[:, :128]
    for k in range(1, x.shape[1] // 128):
        folded = op(folded, x[:, k * 128 : (k + 1) * 128])
    return folded


def attend(queries, keys, values, usable, scores):
    positions = scores.shape[1]
    step = min(STEP, positions)
    steps = range(0, positions, step)
    highest = None
    for at in steps:
        part = dot_rows(queries, keys(at, step))
        lane = lax.broadcasted_iota(jnp.int32, (1, step), 1) + at
        part = part + jnp.where(lane < usable, 0.0, NEG)
        scores[:, at : at + step] = part
        folded = lanes_folded(part, jnp.maximum)
        highest = folded if highest is None else jnp.maximum(highest, folded)
    highest = jnp.max(highest, axis=1, keepdims=True)
    total = jnp.zeros((queries.shape[0], 128), f32)
    weighted = jnp.zeros((queries.shape[0], HD), f32)
    for at in steps:
        weights = jnp.exp2((scores[:, at : at + step] - highest) * SCALE_2).astype(bf16)
        total = total + lanes_folded(weights.astype(f32), jnp.add)
        weighted = weighted + dot(weights, values(at, step))
    return highest * SCALE, jnp.sum(total, axis=1, keepdims=True), weighted


def partials_kernel(
    lengths,
    hidden,
    w_kv,
    queries_draft,
    queries_verify,
    keys,
    values,
    key_levels,
    value_levels,
    key_scales,
    value_scales,
    message,
    scores,
    sums,
    stats,
    fresh,
    stage,
):
    b = pl.program_id(0)
    local_len = keys.shape[2]

    @pl.when(b == 0)
    def _():
        part = dot(hidden[...].reshape(ROUNDS * BATCH * R, hidden.shape[2]), w_kv[...])
        for k in range(BATCH):
            for kv in range(2):
                for t in range(ROUNDS):
                    fresh[k, kv * NEW + t * R : kv * NEW + (t + 1) * R] = part[
                        (t * BATCH + k) * R : (t * BATCH + k + 1) * R, kv * HD : (kv + 1) * HD
                    ]

    usable = jnp.clip(lengths[b] - lax.axis_index("seq") * local_len, 0, local_len)
    lane = lax.broadcasted_iota(jnp.int32, (ROWS, 128), 1)

    @pl.when(usable == 0)
    def _():
        sums[...] = jnp.zeros_like(sums)
        stats[...] = jnp.where(
            lax.broadcasted_iota(jnp.int32, stats.shape, 1) == 0, NEG, 0.0
        )

    @pl.when(usable > 0)
    def _():
        def expanded(levels, scales):
            columns = scales[0].T

            def rows(at, step):
                parts = [
                    (levels[0, 0, k : k + 128].astype(f32) * columns[:, k // 128 : k // 128 + 1]).astype(bf16)
                    for k in range(at, at + step, 128)
                ]
                return jnp.concatenate(parts, axis=0)

            return rows

        def plain(cache):
            return lambda at, step: cache[0, 0, at : at + step]

        draft = (queries_draft, expanded(key_levels, key_scales), expanded(value_levels, value_scales))
        verify = (queries_verify, plain(keys), plain(values))
        for kind, (queries, key_rows, value_rows) in enumerate((draft, verify)):
            rows = queries[...].reshape(ROWS, HD)
            maxima, totals, weighted = attend(rows, key_rows, value_rows, usable, scores.at[kind])
            sums[kind * ROWS : (kind + 1) * ROWS] = weighted
            stats[kind * ROWS : (kind + 1) * ROWS] = jnp.where(lane == 0, maxima, totals)

    pieces = [
        (g, kt * R, kt * GROUP * R + g * R) for g in range(GROUP) for kt in range(KINDS * ROUNDS)
    ]
    ordered = []
    for g, to, at in pieces:
        stage[g, to : to + R] = sums[at : at + R]
        ordered.append(stats[at : at + R])
    turned = jnp.concatenate(
        [jnp.concatenate(ordered, axis=0), jnp.zeros((256 - KINDS * ROWS, 128), f32)], axis=0
    ).T
    maxima, totals = turned[0:1], turned[1:2]
    parts = []
    for x in (maxima, totals):
        high = rounded(x)
        middle = rounded(x - high)
        parts += [high, middle, x - high - middle]
    parts = jnp.concatenate(parts + [jnp.zeros((2, 256), f32)], axis=0)
    high = rounded(fresh[b])
    low = fresh[b] - high
    for g in range(GROUP):
        stage[g, AT_STATS:AT_HIGH] = jnp.zeros((8, 128), f32)
        stage[g, AT_STATS:AT_HIGH, :SHARE] = parts[:, g * SHARE : (g + 1) * SHARE]
        stage[g, AT_HIGH:AT_LOW] = high
        stage[g, AT_LOW:] = low
    message[:, 0] = stage[...].astype(bf16)


def partials(hidden, w_kv, queries_draft, queries_verify, caches, scales, lengths):
    local_len = caches[0].shape[2]

    def whole(shape):
        return pl.BlockSpec(shape, lambda b, lengths: (0,) * len(shape))

    queries = pl.BlockSpec((ROUNDS, 1, 1, GROUP * R, HD), lambda b, lengths: (0, b, 0, 0, 0))
    cache = pl.BlockSpec((1, 1, local_len, HD), lambda b, lengths: (b, 0, 0, 0))
    scale = pl.BlockSpec((1, local_len // 128, 128), lambda b, lengths: (b, 0, 0))
    return pl.pallas_call(
        partials_kernel,
        out_shape=jax.ShapeDtypeStruct((GROUP, BATCH, MESSAGE, HD), bf16),
        grid_spec=pltpu.PrefetchScalarGridSpec(
            num_scalar_prefetch=1,
            grid=(BATCH,),
            in_specs=[whole(hidden.shape), whole(w_kv.shape), queries, queries]
            + [cache] * 4
            + [scale] * 2,
            out_specs=pl.BlockSpec((GROUP, 1, MESSAGE, HD), lambda b, lengths: (0, b, 0, 0)),
            scratch_shapes=[
                pltpu.VMEM((KINDS, ROWS, local_len), f32),
                pltpu.VMEM((KINDS * ROWS, HD), f32),
                pltpu.VMEM((KINDS * ROWS, 128), f32),
                pltpu.VMEM((BATCH, 2 * NEW, HD), f32),
                pltpu.VMEM((GROUP, MESSAGE, HD), f32),
            ],
        ),
        compiler_params=pltpu.CompilerParams(vmem_limit_bytes=VMEM_LIMIT),
        name="partials",
    )(lengths, hidden, w_kv, queries_draft, queries_verify, *caches, *scales)


def joined_kernel(accepted, received, queries_draft, queries_verify, copies):
    peers = received.shape[0]
    index = lax.axis_index("seq")
    g, b = index // BATCH, index % BATCH
    groups = [q[t, b, 0] for q in (queries_draft, queries_verify) for t in range(ROUNDS)]
    row = lax.broadcasted_iota(jnp.int32, (SHARE, KINDS * ROWS), 0)
    column = lax.broadcasted_iota(jnp.int32, (SHARE, KINDS * ROWS), 1)
    chosen = ((column >> 5) == (row >> 2)) & ((column & 31) == g * R + (row & 3))
    queries = dot(jnp.where(chosen, 1.0, 0.0).astype(bf16), jnp.concatenate(groups, axis=0)).astype(bf16)

    new = jnp.zeros((2 * 2 * NEW, HD), f32)
    for s in range(peers):
        new = new + received[s, AT_HIGH:MESSAGE].astype(f32)
    new = (new[: 2 * NEW] + new[2 * NEW :]).astype(bf16).astype(f32)
    new_keys = new[:16].astype(bf16)
    new_values = jnp.concatenate([new[NEW : 2 * NEW], jnp.zeros((16 - NEW, HD), f32)], axis=0).astype(bf16)
    row = lax.broadcasted_iota(jnp.int32, (SHARE, 16), 0)
    column = lax.broadcasted_iota(jnp.int32, (SHARE, 16), 1)
    turn = row >> 2
    turn = jnp.where(turn >= ROUNDS, turn - ROUNDS, turn)
    written, place = column >> 2, column & 3
    kept = jnp.where(written == 0, accepted[0, b], jnp.where(written == 1, accepted[1, b], 0))
    visible = ((written < turn) & (place < kept)) | ((written == turn) & (place <= (row & 3)))
    scores = jnp.where(visible, dot_rows(queries, new_keys) * SCALE, NEG)
    new_maxima = jnp.max(scores, axis=1, keepdims=True)
    weights = jnp.where(visible, jnp.exp(scores - new_maxima), 0.0).astype(bf16)
    new_totals = jnp.sum(weights.astype(f32), axis=1, keepdims=True)
    new_sums = dot(weights, new_values)

    stats = received[:, 16:32].astype(f32)[:, AT_STATS - 16 :]
    maxima = stats[:, 0] + (stats[:, 1] + stats[:, 2])
    totals = stats[:, 3] + (stats[:, 4] + stats[:, 5])
    highest = jnp.max(maxima, axis=0, keepdims=True)
    factors = jnp.exp(maxima - highest)
    total = jnp.sum(totals * factors, axis=0, keepdims=True)
    turned = jnp.concatenate(
        [factors, jnp.broadcast_to(highest, (8, 128)), jnp.broadcast_to(total, (8, 128))], axis=0
    ).T[:SHARE]
    sums = jnp.zeros((SHARE, HD), f32)
    for s in range(peers):
        sums = sums + turned[:, s : s + 1] * received[s, :32].astype(f32)[:SHARE]
    highest, total = turned[:, peers : peers + 1], turned[:, peers + 8 : peers + 9]
    overall = jnp.maximum(highest, new_maxima)
    factor, new_factor = jnp.exp(highest - overall), jnp.exp(new_maxima - overall)
    attended = (sums * factor + new_sums * new_factor) / (total * factor + new_totals * new_factor)
    attended = attended.astype(bf16)
    for s in range(peers):
        copies[s] = attended


def projected_kernel(received, w_out, copies):
    rows = received[...].astype(f32)
    share = [
        rows[g * BATCH : (g + 1) * BATCH].reshape(TOKENS, HD).astype(bf16) for g in range(GROUP)
    ]
    out = dot(jnp.concatenate(share, axis=1), w_out[...]).astype(bf16)
    for k in range(copies.shape[0]):
        copies[k] = out


def summed_kernel(received, out):
    total = received[0].astype(f32)
    for k in range(1, received.shape[0]):
        total = total + received[k].astype(f32)
    row = lax.broadcasted_iota(jnp.int32, (TOKENS, TOKENS), 0)
    column = lax.broadcasted_iota(jnp.int32, (TOKENS, TOKENS), 1)
    at = row >> 2
    t, kind, b = at >> 3, (at >> 2) & 1, at & 3
    source = (b * KINDS * ROUNDS + kind * ROUNDS + t) * R + (row & 3)
    order = jnp.where(column == source, 1.0, 0.0).astype(bf16)
    ordered = dot(order, total.astype(bf16)).astype(bf16)
    out[...] = ordered.reshape(out.shape)


def in_vmem(count):
    return [pl.BlockSpec(memory_space=pltpu.VMEM)] * count


def per_device(
    hidden_new,
    w_kv,
    w_out,
    queries_draft,
    queries_verify,
    keys_cache,
    values_cache,
    key_levels,
    value_levels,
    key_scales,
    value_scales,
    lengths,
    accepted,
):
    peers, heads = lax.axis_size("seq"), lax.axis_size("tp")
    params = pltpu.CompilerParams(vmem_limit_bytes=VMEM_LIMIT)
    scales = [x.reshape(BATCH, -1, 128) for x in (key_scales, value_scales)]
    message = partials(
        hidden_new,
        w_kv.reshape(w_kv.shape[0], -1),
        queries_draft,
        queries_verify,
        (keys_cache, values_cache, key_levels, value_levels),
        scales,
        lengths,
    ).reshape(peers, MESSAGE, HD)
    received = lax.all_to_all(message, "seq", 0, 0, tiled=True)
    copies = pl.pallas_call(
        joined_kernel,
        out_shape=jax.ShapeDtypeStruct((peers, SHARE, HD), bf16),
        in_specs=[pl.BlockSpec(memory_space=pltpu.SMEM)] + in_vmem(3),
        out_specs=pl.BlockSpec(memory_space=pltpu.VMEM),
        compiler_params=params,
        name="joined",
    )(accepted, received, queries_draft, queries_verify)
    received = lax.all_to_all(copies, "seq", 0, 0, tiled=True)
    copies = pl.pallas_call(
        projected_kernel,
        out_shape=jax.ShapeDtypeStruct((heads, TOKENS, w_out.shape[1]), bf16),
        in_specs=in_vmem(2),
        out_specs=pl.BlockSpec(memory_space=pltpu.VMEM),
        compiler_params=params,
        name="projected",
    )(received, w_out)
    received = lax.all_to_all(copies, "tp", 0, 0, tiled=True)
    return pl.pallas_call(
        summed_kernel,
        out_shape=jax.ShapeDtypeStruct((ROUNDS, KINDS, BATCH * R, w_out.shape[1]), bf16),
        in_specs=in_vmem(1),
        out_specs=pl.BlockSpec(memory_space=pltpu.VMEM),
        compiler_params=params,
        name="summed",
    )(received)


def solution(mesh):
    in_specs = (
        P(None, None, "seq"),
        P("seq", "tp", None),
        P("tp", "seq"),
        P(None, None, "tp", None, None),
        P(None, None, "tp", None, None),
        P(None, "tp", "seq", None),
        P(None, "tp", "seq", None),
        P(None, "tp", "seq", None),
        P(None, "tp", "seq", None),
        P(None, "tp", "seq"),
        P(None, "tp", "seq"),
        P(),
        P(),
    )
    return jax.shard_map(
        per_device,
        mesh=mesh,
        in_specs=in_specs,
        out_specs=P(None, None, None, "seq"),
        check_vma=False,
    )
```

```python
import math

import jax
import jax.numpy as jnp
from jax import lax
from jax.experimental import pallas as pl
from jax.experimental.pallas import tpu as pltpu
from jax.sharding import PartitionSpec as P

HD = 128
GROUP = 8
R = 4
ROUNDS = 3
BATCH = 4
KINDS = 2
NEG = -1e30
SCALE = 1.0 / math.sqrt(HD)
SCALE_2 = SCALE / math.log(2.0)
ROWS = ROUNDS * GROUP * R
SHARE = KINDS * ROUNDS * R
NEW = ROUNDS * R
TOKENS = KINDS * ROUNDS * BATCH * R
AT_STATS = SHARE
AT_HIGH = SHARE + 8
AT_LOW = AT_HIGH + 2 * NEW
MESSAGE = AT_LOW + 2 * NEW
STEP = 512
FEW = 256
VMEM_LIMIT = 48 * 1024 * 1024

f32 = jnp.float32
bf16 = jnp.bfloat16


def rounded(x):
    return x.astype(bf16).astype(f32)


def dot(a, b):
    return jnp.dot(a, b, preferred_element_type=f32)


def dot_rows(a, b):
    return lax.dot_general(a, b, (((1,), (1,)), ((), ())), preferred_element_type=f32)


def lanes_folded(x, op):
    folded = x[:, :128]
    for k in range(1, x.shape[1] // 128):
        folded = op(folded, x[:, k * 128 : (k + 1) * 128])
    return folded


def attend(queries, keys, values, usable, scores, positions):
    step = min(STEP, positions)
    steps = range(0, positions, step)
    highest = None
    for at in steps:
        part = dot_rows(queries, keys[at : at + step])
        lane = lax.broadcasted_iota(jnp.int32, (1, step), 1) + at
        part = part + jnp.where(lane < usable, 0.0, NEG)
        scores[:, at : at + step] = part
        folded = lanes_folded(part, jnp.maximum)
        highest = folded if highest is None else jnp.maximum(highest, folded)
    highest = jnp.max(highest, axis=1, keepdims=True)
    total = jnp.zeros((queries.shape[0], 128), f32)
    weighted = jnp.zeros((queries.shape[0], KINDS * HD), f32)
    for at in steps:
        weights = jnp.exp2((scores[:, at : at + step] - highest) * SCALE_2).astype(bf16)
        total = total + lanes_folded(weights.astype(f32), jnp.add)
        weighted = weighted + dot(weights, values[at : at + step])
    return highest * SCALE, jnp.sum(total, axis=1, keepdims=True), weighted


def partials_kernel(
    lengths_hbm,
    hidden_hbm,
    w_kv_hbm,
    queries_draft_hbm,
    queries_verify_hbm,
    keys_hbm,
    values_hbm,
    key_levels_hbm,
    value_levels_hbm,
    key_scales_hbm,
    value_scales_hbm,
    message,
    lengths,
    hidden,
    w_kv,
    queries_draft,
    queries_verify,
    keys,
    values,
    key_levels,
    value_levels,
    key_scales,
    value_scales,
    scores,
    sums,
    stats,
    fresh,
    stage,
    small_sems,
    cache_sems,
):
    local_len = keys.shape[1]
    few = min(FEW, local_len)
    small = [
        pltpu.make_async_copy(source, target, small_sems.at[k])
        for k, (source, target) in enumerate(
            (
                (lengths_hbm, lengths),
                (queries_draft_hbm, queries_draft),
                (queries_verify_hbm, queries_verify),
                (key_scales_hbm, key_scales),
                (value_scales_hbm, value_scales),
                (hidden_hbm, hidden),
                (w_kv_hbm, w_kv),
            )
        )
    ]
    for copy in small:
        copy.start()
    small[0].wait()
    first = lax.axis_index("seq") * local_len

    def usable_of(b):
        return jnp.clip(lengths[b] - first, 0, local_len)

    def cache_copies(b, rows):
        at = pl.ds(0, rows)
        return [
            pltpu.make_async_copy(key_levels_hbm.at[b, 0, at], key_levels.at[b, at], cache_sems.at[b, 0]),
            pltpu.make_async_copy(keys_hbm.at[b, 0, at], keys.at[b, at, pl.ds(HD, HD)], cache_sems.at[b, 1]),
            pltpu.make_async_copy(value_levels_hbm.at[b, 0, at], value_levels.at[b, at], cache_sems.at[b, 2]),
            pltpu.make_async_copy(values_hbm.at[b, 0, at], values.at[b, at, pl.ds(HD, HD)], cache_sems.at[b, 3]),
        ]

    for b in range(BATCH):
        usable = usable_of(b)

        @pl.when(usable > few)
        def _():
            for copy in cache_copies(b, local_len):
                copy.start()

        @pl.when((usable > 0) & (usable <= few))
        def _():
            for copy in cache_copies(b, few):
                copy.start()

    for copy in small[1:]:
        copy.wait()
    part = dot(hidden[...].reshape(ROUNDS * BATCH * R, hidden.shape[2]), w_kv[...])
    for k in range(BATCH):
        for kv in range(2):
            for t in range(ROUNDS):
                fresh[k, kv * NEW + t * R : kv * NEW + (t + 1) * R] = part[
                    (t * BATCH + k) * R : (t * BATCH + k + 1) * R, kv * HD : (kv + 1) * HD
                ]

    lane = lax.broadcasted_iota(jnp.int32, (KINDS * ROWS, 128), 1)
    pieces = [
        (g, kt * R, kt * GROUP * R + g * R) for g in range(GROUP) for kt in range(KINDS * ROUNDS)
    ]

    def sequence(b, _):
        usable = usable_of(b)

        def over(positions):
            copies = cache_copies(b, positions)
            for levels, scales, target, ready in (
                (key_levels, key_scales, keys, copies[:2]),
                (value_levels, value_scales, values, copies[2:]),
            ):
                columns = scales[b].T
                for copy in ready:
                    copy.wait()
                for k in range(positions // 128):
                    at = pl.ds(k * 128, 128)
                    low = levels[b, at].astype(f32) * columns[:, k : k + 1]
                    target[b, at, :HD] = low.astype(bf16)
            zeros = jnp.zeros((ROWS, HD), bf16)
            rows = jnp.concatenate(
                [
                    jnp.concatenate([queries_draft[:, b, 0].reshape(ROWS, HD), zeros], axis=1),
                    jnp.concatenate([zeros, queries_verify[:, b, 0].reshape(ROWS, HD)], axis=1),
                ],
                axis=0,
            )
            maxima, totals, weighted = attend(rows, keys.at[b], values.at[b], usable, scores, positions)
            sums[:ROWS] = weighted[:ROWS, :HD]
            sums[ROWS:] = weighted[ROWS:, HD:]
            stats[...] = jnp.where(lane == 0, maxima, totals)

        @pl.when(usable == 0)
        def _():
            sums[...] = jnp.zeros_like(sums)
            stats[...] = jnp.where(lane == 0, NEG, 0.0)

        @pl.when((usable > 0) & (usable <= few))
        def _():
            over(few)

        @pl.when(usable > few)
        def _():
            over(local_len)

        ordered = []
        for g, to, at in pieces:
            stage[g, to : to + R] = sums[at : at + R]
            ordered.append(stats[at : at + R])
        turned = jnp.concatenate(
            [jnp.concatenate(ordered, axis=0), jnp.zeros((256 - KINDS * ROWS, 128), f32)], axis=0
        ).T
        parts = []
        for x in (turned[0:1], turned[1:2]):
            high = rounded(x)
            middle = rounded(x - high)
            parts += [high, middle, x - high - middle]
        parts = jnp.concatenate(parts + [jnp.zeros((2, 256), f32)], axis=0)
        high = rounded(fresh[b])
        low = fresh[b] - high
        for g in range(GROUP):
            stage[g, AT_STATS:AT_HIGH] = jnp.zeros((8, 128), f32)
            stage[g, AT_STATS:AT_HIGH, :SHARE] = parts[:, g * SHARE : (g + 1) * SHARE]
            stage[g, AT_HIGH:AT_LOW] = high
            stage[g, AT_LOW:] = low
        message[:, b] = stage[...].astype(bf16)
        return 0

    lax.fori_loop(0, BATCH, sequence, 0)


def partials(lengths, *arrays):
    local_len = arrays[4].shape[2]
    hidden, w_kv, queries = arrays[:3]
    blocks = local_len // 128
    return pl.pallas_call(
        partials_kernel,
        out_shape=jax.ShapeDtypeStruct((GROUP, BATCH, MESSAGE, HD), bf16),
        in_specs=[pl.BlockSpec(memory_space=pltpu.HBM)] * (1 + len(arrays)),
        out_specs=pl.BlockSpec(memory_space=pltpu.VMEM),
        scratch_shapes=[
            pltpu.SMEM((BATCH,), jnp.int32),
            pltpu.VMEM(hidden.shape, bf16),
            pltpu.VMEM(w_kv.shape, bf16),
            pltpu.VMEM(queries.shape, bf16),
            pltpu.VMEM(queries.shape, bf16),
            pltpu.VMEM((BATCH, local_len, KINDS * HD), bf16),
            pltpu.VMEM((BATCH, local_len, KINDS * HD), bf16),
            pltpu.VMEM((BATCH, local_len, HD), bf16),
            pltpu.VMEM((BATCH, local_len, HD), bf16),
            pltpu.VMEM((BATCH, blocks, 128), f32),
            pltpu.VMEM((BATCH, blocks, 128), f32),
            pltpu.VMEM((KINDS * ROWS, local_len), f32),
            pltpu.VMEM((KINDS * ROWS, HD), f32),
            pltpu.VMEM((KINDS * ROWS, 128), f32),
            pltpu.VMEM((BATCH, 2 * NEW, HD), f32),
            pltpu.VMEM((GROUP, MESSAGE, HD), f32),
            pltpu.SemaphoreType.DMA((7,)),
            pltpu.SemaphoreType.DMA((BATCH, 4)),
        ],
        compiler_params=pltpu.CompilerParams(vmem_limit_bytes=VMEM_LIMIT),
        name="partials",
    )(*(pltpu.with_memory_space_constraint(x, pltpu.HBM) for x in (lengths, *arrays)))


def joined_kernel(accepted, received, queries_draft, queries_verify, copies):
    peers = received.shape[0]
    index = lax.axis_index("seq")
    g, b = index // BATCH, index % BATCH
    groups = [q[t, b, 0] for q in (queries_draft, queries_verify) for t in range(ROUNDS)]
    row = lax.broadcasted_iota(jnp.int32, (SHARE, KINDS * ROWS), 0)
    column = lax.broadcasted_iota(jnp.int32, (SHARE, KINDS * ROWS), 1)
    chosen = ((column >> 5) == (row >> 2)) & ((column & 31) == g * R + (row & 3))
    queries = dot(jnp.where(chosen, 1.0, 0.0).astype(bf16), jnp.concatenate(groups, axis=0)).astype(bf16)

    new = jnp.zeros((2 * 2 * NEW, HD), f32)
    for s in range(peers):
        new = new + received[s, AT_HIGH:MESSAGE].astype(f32)
    new = (new[: 2 * NEW] + new[2 * NEW :]).astype(bf16).astype(f32)
    new_keys = new[:16].astype(bf16)
    new_values = jnp.concatenate([new[NEW : 2 * NEW], jnp.zeros((16 - NEW, HD), f32)], axis=0).astype(bf16)
    row = lax.broadcasted_iota(jnp.int32, (SHARE, 16), 0)
    column = lax.broadcasted_iota(jnp.int32, (SHARE, 16), 1)
    turn = row >> 2
    turn = jnp.where(turn >= ROUNDS, turn - ROUNDS, turn)
    written, place = column >> 2, column & 3
    kept = jnp.where(written == 0, accepted[0, b], jnp.where(written == 1, accepted[1, b], 0))
    visible = ((written < turn) & (place < kept)) | ((written == turn) & (place <= (row & 3)))
    scores = jnp.where(visible, dot_rows(queries, new_keys) * SCALE, NEG)
    new_maxima = jnp.max(scores, axis=1, keepdims=True)
    weights = jnp.where(visible, jnp.exp(scores - new_maxima), 0.0).astype(bf16)
    new_totals = jnp.sum(weights.astype(f32), axis=1, keepdims=True)
    new_sums = dot(weights, new_values)

    stats = received[:, 16:32].astype(f32)[:, AT_STATS - 16 :]
    maxima = stats[:, 0] + (stats[:, 1] + stats[:, 2])
    totals = stats[:, 3] + (stats[:, 4] + stats[:, 5])
    highest = jnp.max(maxima, axis=0, keepdims=True)
    factors = jnp.exp(maxima - highest)
    total = jnp.sum(totals * factors, axis=0, keepdims=True)
    turned = jnp.concatenate(
        [factors, jnp.broadcast_to(highest, (8, 128)), jnp.broadcast_to(total, (8, 128))], axis=0
    ).T[:SHARE]
    sums = jnp.zeros((SHARE, HD), f32)
    for s in range(peers):
        sums = sums + turned[:, s : s + 1] * received[s, :32].astype(f32)[:SHARE]
    highest, total = turned[:, peers : peers + 1], turned[:, peers + 8 : peers + 9]
    overall = jnp.maximum(highest, new_maxima)
    factor, new_factor = jnp.exp(highest - overall), jnp.exp(new_maxima - overall)
    attended = (sums * factor + new_sums * new_factor) / (total * factor + new_totals * new_factor)
    attended = attended.astype(bf16)
    for s in range(peers):
        copies[s] = attended


def projected_kernel(received, w_out, copies):
    rows = received[...].astype(f32)
    share = [
        rows[g * BATCH : (g + 1) * BATCH].reshape(TOKENS, HD).astype(bf16) for g in range(GROUP)
    ]
    out = dot(jnp.concatenate(share, axis=1), w_out[...]).astype(bf16)
    for k in range(copies.shape[0]):
        copies[k] = out


def summed_kernel(received, out):
    total = received[0].astype(f32)
    for k in range(1, received.shape[0]):
        total = total + received[k].astype(f32)
    row = lax.broadcasted_iota(jnp.int32, (TOKENS, TOKENS), 0)
    column = lax.broadcasted_iota(jnp.int32, (TOKENS, TOKENS), 1)
    at = row >> 2
    t, kind, b = at >> 3, (at >> 2) & 1, at & 3
    source = (b * KINDS * ROUNDS + kind * ROUNDS + t) * R + (row & 3)
    order = jnp.where(column == source, 1.0, 0.0).astype(bf16)
    ordered = dot(order, total.astype(bf16)).astype(bf16)
    out[...] = ordered.reshape(out.shape)


def in_vmem(count):
    return [pl.BlockSpec(memory_space=pltpu.VMEM)] * count


def per_device(
    hidden_new,
    w_kv,
    w_out,
    queries_draft,
    queries_verify,
    keys_cache,
    values_cache,
    key_levels,
    value_levels,
    key_scales,
    value_scales,
    lengths,
    accepted,
):
    peers, heads = lax.axis_size("seq"), lax.axis_size("tp")
    params = pltpu.CompilerParams(vmem_limit_bytes=VMEM_LIMIT)
    scales = [x.reshape(BATCH, -1, 128) for x in (key_scales, value_scales)]
    message = partials(
        lengths,
        hidden_new,
        w_kv.reshape(w_kv.shape[0], -1),
        queries_draft,
        queries_verify,
        keys_cache,
        values_cache,
        key_levels,
        value_levels,
        *scales,
    ).reshape(peers, MESSAGE, HD)
    received = lax.all_to_all(message, "seq", 0, 0, tiled=True)
    copies = pl.pallas_call(
        joined_kernel,
        out_shape=jax.ShapeDtypeStruct((peers, SHARE, HD), bf16),
        in_specs=[pl.BlockSpec(memory_space=pltpu.SMEM)] + in_vmem(3),
        out_specs=pl.BlockSpec(memory_space=pltpu.VMEM),
        compiler_params=params,
        name="joined",
    )(accepted, received, queries_draft, queries_verify)
    received = lax.all_to_all(copies, "seq", 0, 0, tiled=True)
    copies = pl.pallas_call(
        projected_kernel,
        out_shape=jax.ShapeDtypeStruct((heads, TOKENS, w_out.shape[1]), bf16),
        in_specs=in_vmem(2),
        out_specs=pl.BlockSpec(memory_space=pltpu.VMEM),
        compiler_params=params,
        name="projected",
    )(received, w_out)
    received = lax.all_to_all(copies, "tp", 0, 0, tiled=True)
    return pl.pallas_call(
        summed_kernel,
        out_shape=jax.ShapeDtypeStruct((ROUNDS, KINDS, BATCH * R, w_out.shape[1]), bf16),
        in_specs=in_vmem(1),
        out_specs=pl.BlockSpec(memory_space=pltpu.VMEM),
        compiler_params=params,
        name="summed",
    )(received)


def solution(mesh):
    in_specs = (
        P(None, None, "seq"),
        P("seq", "tp", None),
        P("tp", "seq"),
        P(None, None, "tp", None, None),
        P(None, None, "tp", None, None),
        P(None, "tp", "seq", None),
        P(None, "tp", "seq", None),
        P(None, "tp", "seq", None),
        P(None, "tp", "seq", None),
        P(None, "tp", "seq"),
        P(None, "tp", "seq"),
        P(),
        P(),
    )
    return jax.shard_map(
        per_device,
        mesh=mesh,
        in_specs=in_specs,
        out_specs=P(None, None, None, "seq"),
        check_vma=False,
    )
```

```python
import math

import jax
import jax.numpy as jnp
from jax import lax
from jax.experimental import pallas as pl
from jax.experimental.pallas import tpu as pltpu
from jax.sharding import PartitionSpec as P

HD = 128
GROUP = 8
R = 4
ROUNDS = 3
BATCH = 4
KINDS = 2
NEG = -1e30
SCALE = 1.0 / math.sqrt(HD)
SCALE_2 = SCALE / math.log(2.0)
ROWS = ROUNDS * GROUP * R
SHARE = KINDS * ROUNDS * R
NEW = ROUNDS * R
TOKENS = KINDS * ROUNDS * BATCH * R
TAIL = SHARE
PIECE = 3
MESSAGE = SHARE + 8
STEP = 512
FEW = 256
VMEM_LIMIT = 48 * 1024 * 1024

f32 = jnp.float32
bf16 = jnp.bfloat16


def rounded(x):
    return x.astype(bf16).astype(f32)


def dot(a, b):
    return jnp.dot(a, b, preferred_element_type=f32)


def dot_rows(a, b):
    return lax.dot_general(a, b, (((1,), (1,)), ((), ())), preferred_element_type=f32)


def parted(x):
    high = rounded(x)
    middle = rounded(x - high)
    return high, middle, x - high - middle


def by_head():
    row = lax.broadcasted_iota(jnp.int32, (KINDS * ROWS, KINDS * ROWS), 0)
    column = lax.broadcasted_iota(jnp.int32, (KINDS * ROWS, KINDS * ROWS), 1)
    target = ((column >> 2) & 7) * SHARE + ((column >> 5) << 2) + (column & 3)
    return jnp.where(row == target, 1.0, 0.0).astype(bf16)


def stats_spread(maxima, totals, place):
    lane = lax.broadcasted_iota(jnp.int32, (1, 128), 1)
    part = sum(jnp.where(lane >= k * SHARE, 1, 0) for k in range(1, 5))
    spread = jnp.zeros((maxima.shape[0], 128), f32)
    for k, x in enumerate(parted(maxima) + parted(totals)[:2]):
        spread = jnp.where(part == k, x, spread)
    return jnp.where(lane - part * SHARE == place, spread, 0.0)


def stats_of(rows):
    turned = rows.T
    parts = [turned[k * SHARE : (k + 1) * SHARE] for k in range(5)]
    return parts[0] + (parts[1] + parts[2]), parts[3] + parts[4]


def tails_of(received):
    return received[:, TAIL - 8 :].astype(f32)[:, 8:]


def lanes_folded(x, op):
    folded = x[:, :128]
    for k in range(1, x.shape[1] // 128):
        folded = op(folded, x[:, k * 128 : (k + 1) * 128])
    return folded


def attend(queries, keys, values, usable, scores, positions):
    step = min(STEP, positions)
    steps = range(0, positions, step)
    highest = None
    for at in steps:
        part = dot_rows(queries, keys[at : at + step])
        lane = lax.broadcasted_iota(jnp.int32, (1, step), 1) + at
        part = part + jnp.where(lane < usable, 0.0, NEG)
        scores[:, at : at + step] = part
        folded = lanes_folded(part, jnp.maximum)
        highest = folded if highest is None else jnp.maximum(highest, folded)
    highest = jnp.max(highest, axis=1, keepdims=True)
    total = jnp.zeros((queries.shape[0], 128), f32)
    weighted = jnp.zeros((queries.shape[0], KINDS * HD), f32)
    for at in steps:
        weights = jnp.exp2((scores[:, at : at + step] - highest) * SCALE_2).astype(bf16)
        total = total + lanes_folded(weights.astype(f32), jnp.add)
        weighted = weighted + dot(weights, values[at : at + step])
    return highest * SCALE, jnp.sum(total, axis=1, keepdims=True), weighted


def partials_kernel(
    lengths_hbm,
    hidden_hbm,
    w_kv_hbm,
    queries_draft_hbm,
    queries_verify_hbm,
    keys_hbm,
    values_hbm,
    key_levels_hbm,
    value_levels_hbm,
    key_scales_hbm,
    value_scales_hbm,
    message,
    lengths,
    hidden,
    w_kv,
    queries_draft,
    queries_verify,
    keys,
    values,
    key_levels,
    value_levels,
    key_scales,
    value_scales,
    scores,
    sums,
    stats,
    order,
    tails,
    small_sems,
    cache_sems,
):
    local_len = keys.shape[1]
    few = min(FEW, local_len)
    small = [
        pltpu.make_async_copy(source, target, small_sems.at[k])
        for k, (source, target) in enumerate(
            (
                (lengths_hbm, lengths),
                (queries_draft_hbm, queries_draft),
                (queries_verify_hbm, queries_verify),
                (key_scales_hbm, key_scales),
                (value_scales_hbm, value_scales),
                (hidden_hbm, hidden),
                (w_kv_hbm, w_kv),
            )
        )
    ]
    for copy in small:
        copy.start()
    small[0].wait()
    first = lax.axis_index("seq") * local_len

    def usable_of(b):
        return jnp.clip(lengths[b] - first, 0, local_len)

    def cache_copies(b, rows):
        at = pl.ds(0, rows)
        return [
            pltpu.make_async_copy(key_levels_hbm.at[b, 0, at], key_levels.at[b, at], cache_sems.at[b, 0]),
            pltpu.make_async_copy(keys_hbm.at[b, 0, at], keys.at[b, at, pl.ds(HD, HD)], cache_sems.at[b, 1]),
            pltpu.make_async_copy(value_levels_hbm.at[b, 0, at], value_levels.at[b, at], cache_sems.at[b, 2]),
            pltpu.make_async_copy(values_hbm.at[b, 0, at], values.at[b, at, pl.ds(HD, HD)], cache_sems.at[b, 3]),
        ]

    for b in range(BATCH):
        usable = usable_of(b)

        @pl.when(usable > few)
        def _():
            for copy in cache_copies(b, local_len):
                copy.start()

        @pl.when((usable > 0) & (usable <= few))
        def _():
            for copy in cache_copies(b, few):
                copy.start()

    for copy in small[1:]:
        copy.wait()
    part = dot(hidden[...].reshape(ROUNDS * BATCH * R, hidden.shape[2]), w_kv[...])
    part = jnp.concatenate([part[:, :HD], part[:, HD:]], axis=0)
    row = lax.broadcasted_iota(jnp.int32, (GROUP * BATCH * 8, 2 * TOKENS // KINDS), 0)
    column = lax.broadcasted_iota(jnp.int32, (GROUP * BATCH * 8, 2 * TOKENS // KINDS), 1)
    source = (row >> 3) * PIECE + (row & 7) - 1
    high = part.astype(bf16)
    low = (part - high.astype(f32)).astype(bf16)
    to_high = ((row & 7) >= 1) & ((row & 7) <= PIECE) & (column == source)
    to_low = ((row & 7) > PIECE) & ((row & 7) <= 2 * PIECE) & (column == source - PIECE)
    tails[...] = (
        dot(jnp.where(to_high, 1.0, 0.0).astype(bf16), high)
        + dot(jnp.where(to_low, 1.0, 0.0).astype(bf16), low)
    ).reshape(tails.shape)
    order[...] = by_head()

    row = lax.broadcasted_iota(jnp.int32, (KINDS * ROWS, 1), 0)
    place = ((row >> 5) << 2) + (row & 3)
    row = lax.broadcasted_iota(jnp.int32, (GROUP, KINDS * ROWS), 0)
    column = lax.broadcasted_iota(jnp.int32, (GROUP, KINDS * ROWS), 1)
    of_head = jnp.where(((column >> 2) & 7) == row, 1.0, 0.0).astype(bf16)
    first_row = lax.broadcasted_iota(jnp.int32, (GROUP, 8, 128), 1) == 0

    def sequence(b, _):
        usable = usable_of(b)

        def over(positions):
            copies = cache_copies(b, positions)
            for levels, scales, target, ready in (
                (key_levels, key_scales, keys, copies[:2]),
                (value_levels, value_scales, values, copies[2:]),
            ):
                columns = scales[b].T
                for copy in ready:
                    copy.wait()
                for k in range(positions // 128):
                    at = pl.ds(k * 128, 128)
                    low = levels[b, at].astype(f32) * columns[:, k : k + 1]
                    target[b, at, :HD] = low.astype(bf16)
            zeros = jnp.zeros((ROWS, HD), bf16)
            rows = jnp.concatenate(
                [
                    jnp.concatenate([queries_draft[:, b, 0].reshape(ROWS, HD), zeros], axis=1),
                    jnp.concatenate([zeros, queries_verify[:, b, 0].reshape(ROWS, HD)], axis=1),
                ],
                axis=0,
            )
            maxima, totals, weighted = attend(rows, keys.at[b], values.at[b], usable, scores, positions)
            sums[:ROWS] = weighted[:ROWS, :HD].astype(bf16)
            sums[ROWS:] = weighted[ROWS:, HD:].astype(bf16)
            stats[...] = stats_spread(maxima, totals, place).astype(bf16)

        @pl.when(usable == 0)
        def _():
            sums[...] = jnp.zeros_like(sums)
            none = jnp.zeros((KINDS * ROWS, 1), f32)
            stats[...] = stats_spread(none + NEG, none, place).astype(bf16)

        @pl.when((usable > 0) & (usable <= few))
        def _():
            over(few)

        @pl.when(usable > few)
        def _():
            over(local_len)

        ordered = dot(order[...], sums[...]).reshape(GROUP, SHARE, HD)
        head_stats = dot(of_head, stats[...]).reshape(GROUP, 1, 128)
        tail = jnp.where(first_row, head_stats, tails[:, b])
        message[:, b] = jnp.concatenate([ordered, tail], axis=1).astype(bf16)
        return 0

    lax.fori_loop(0, BATCH, sequence, 0)


def partials(lengths, *arrays):
    local_len = arrays[4].shape[2]
    hidden, w_kv, queries = arrays[:3]
    blocks = local_len // 128
    return pl.pallas_call(
        partials_kernel,
        out_shape=jax.ShapeDtypeStruct((GROUP, BATCH, MESSAGE, HD), bf16),
        in_specs=[pl.BlockSpec(memory_space=pltpu.HBM)] * (1 + len(arrays)),
        out_specs=pl.BlockSpec(memory_space=pltpu.VMEM),
        scratch_shapes=[
            pltpu.SMEM((BATCH,), jnp.int32),
            pltpu.VMEM(hidden.shape, bf16),
            pltpu.VMEM(w_kv.shape, bf16),
            pltpu.VMEM(queries.shape, bf16),
            pltpu.VMEM(queries.shape, bf16),
            pltpu.VMEM((BATCH, local_len, KINDS * HD), bf16),
            pltpu.VMEM((BATCH, local_len, KINDS * HD), bf16),
            pltpu.VMEM((BATCH, local_len, HD), bf16),
            pltpu.VMEM((BATCH, local_len, HD), bf16),
            pltpu.VMEM((BATCH, blocks, 128), f32),
            pltpu.VMEM((BATCH, blocks, 128), f32),
            pltpu.VMEM((KINDS * ROWS, local_len), f32),
            pltpu.VMEM((KINDS * ROWS, HD), bf16),
            pltpu.VMEM((KINDS * ROWS, 128), bf16),
            pltpu.VMEM((KINDS * ROWS, KINDS * ROWS), bf16),
            pltpu.VMEM((GROUP, BATCH, 8, 128), f32),
            pltpu.SemaphoreType.DMA((7,)),
            pltpu.SemaphoreType.DMA((BATCH, 4)),
        ],
        compiler_params=pltpu.CompilerParams(vmem_limit_bytes=VMEM_LIMIT),
        name="partials",
    )(*(pltpu.with_memory_space_constraint(x, pltpu.HBM) for x in (lengths, *arrays)))


def joined_kernel(received, copies):
    peers = received.shape[0]
    tails = tails_of(received)
    maxima, totals = stats_of(tails[:, 0])
    highest = jnp.max(maxima, axis=1, keepdims=True)
    factors = jnp.exp(maxima - highest)
    total = jnp.sum(totals * factors, axis=1, keepdims=True)
    sums = jnp.zeros((SHARE, HD), f32)
    for s in range(peers):
        sums = sums + factors[:, s : s + 1] * received[s].astype(f32)[:SHARE]
    fresh = jnp.sum(tails, axis=0)
    fresh = fresh + jnp.concatenate([fresh[PIECE:], fresh[:PIECE]], axis=0)
    place = lax.broadcasted_iota(jnp.int32, (SHARE, 1), 0)
    stats = jnp.sum(stats_spread(highest, total, place), axis=0, keepdims=True)
    row = lax.broadcasted_iota(jnp.int32, (8, 128), 0)
    tail = jnp.where(row == 0, stats, jnp.where(row <= PIECE, fresh, 0.0))
    block = jnp.concatenate([sums / total, tail], axis=0).astype(bf16)
    for s in range(peers):
        copies[s] = block


def projected_kernel(accepted, received, queries_draft, queries_verify, w_out, copies):
    peers = received.shape[0]
    tails = tails_of(received)
    row = lax.broadcasted_iota(jnp.int32, (BATCH * 2 * 16, peers * 8), 0)
    column = lax.broadcasted_iota(jnp.int32, (BATCH * 2 * 16, peers * 8), 1)
    within = (column & 7) - 1
    source = (column >> 3) * PIECE + within
    kv = jnp.where(source >= TOKENS // KINDS, 1, 0)
    token = source - kv * (TOKENS // KINDS)
    target = ((token >> 2) & 3) * 32 + kv * 16 + ((token >> 4) << 2) + (token & 3)
    chosen = (within >= 0) & (within < PIECE) & (row == target)
    fresh = dot(
        jnp.where(chosen, 1.0, 0.0).astype(bf16), tails.reshape(peers * 8, 128).astype(bf16)
    ).astype(bf16)

    maxima, totals = stats_of(tails[:, 0])
    order = by_head()
    row = lax.broadcasted_iota(jnp.int32, (KINDS * ROWS, 16), 0)
    column = lax.broadcasted_iota(jnp.int32, (KINDS * ROWS, 16), 1)
    turn = (row - ((row * 171) >> 12) * SHARE) >> 2
    turn = jnp.where(turn >= ROUNDS, turn - ROUNDS, turn)
    written, token = column >> 2, column & 3
    itself = (written == turn) & (token <= (row & 3))
    earlier = written < turn
    parts = []
    for b in range(BATCH):
        groups = [q[t, b, 0] for q in (queries_draft, queries_verify) for t in range(ROUNDS)]
        queries = dot(order, jnp.concatenate(groups, axis=0)).astype(bf16)
        kept = jnp.where(written == 0, accepted[0, b], jnp.where(written == 1, accepted[1, b], 0))
        visible = itself | (earlier & (token < kept))
        scores = jnp.where(visible, dot_rows(queries, fresh[b * 32 : b * 32 + 16]) * SCALE, NEG)
        new_highest = jnp.max(scores, axis=1, keepdims=True)
        weights = jnp.where(visible, jnp.exp(scores - new_highest), 0.0).astype(bf16)
        new_total = jnp.sum(weights.astype(f32), axis=1, keepdims=True)
        new_sums = dot(weights, fresh[b * 32 + 16 : b * 32 + 32])
        of_b = range(b, peers, BATCH)
        highest = jnp.concatenate([maxima[:, p : p + 1] for p in of_b], axis=0)
        total = jnp.concatenate([totals[:, p : p + 1] for p in of_b], axis=0)
        means = jnp.concatenate([received[p].astype(f32)[:SHARE] for p in of_b], axis=0)
        overall = jnp.maximum(highest, new_highest)
        factor = total * jnp.exp(highest - overall)
        new_factor = jnp.exp(new_highest - overall)
        whole = factor + new_total * new_factor
        attended = means * (factor / whole) + new_sums * (new_factor / whole)
        parts.append(
            jnp.concatenate([attended[g * SHARE : (g + 1) * SHARE] for g in range(GROUP)], axis=1)
        )
    out = dot(jnp.concatenate(parts, axis=0).astype(bf16), w_out[...]).astype(bf16)
    for k in range(copies.shape[0]):
        copies[k] = out


def summed_kernel(received, out):
    total = received[0].astype(f32)
    for k in range(1, received.shape[0]):
        total = total + received[k].astype(f32)
    row = lax.broadcasted_iota(jnp.int32, (TOKENS, TOKENS), 0)
    column = lax.broadcasted_iota(jnp.int32, (TOKENS, TOKENS), 1)
    at = row >> 2
    t, kind, b = at >> 3, (at >> 2) & 1, at & 3
    source = (b * KINDS * ROUNDS + kind * ROUNDS + t) * R + (row & 3)
    order = jnp.where(column == source, 1.0, 0.0).astype(bf16)
    ordered = dot(order, total.astype(bf16)).astype(bf16)
    out[...] = ordered.reshape(out.shape)


def in_vmem(count):
    return [pl.BlockSpec(memory_space=pltpu.VMEM)] * count


def per_device(
    hidden_new,
    w_kv,
    w_out,
    queries_draft,
    queries_verify,
    keys_cache,
    values_cache,
    key_levels,
    value_levels,
    key_scales,
    value_scales,
    lengths,
    accepted,
):
    peers, heads = lax.axis_size("seq"), lax.axis_size("tp")
    params = pltpu.CompilerParams(vmem_limit_bytes=VMEM_LIMIT)
    scales = [x.reshape(BATCH, -1, 128) for x in (key_scales, value_scales)]
    message = partials(
        lengths,
        hidden_new,
        w_kv.reshape(w_kv.shape[0], -1),
        queries_draft,
        queries_verify,
        keys_cache,
        values_cache,
        key_levels,
        value_levels,
        *scales,
    ).reshape(peers, MESSAGE, HD)
    received = lax.all_to_all(message, "seq", 0, 0, tiled=True)
    copies = pl.pallas_call(
        joined_kernel,
        out_shape=jax.ShapeDtypeStruct((peers, MESSAGE, HD), bf16),
        in_specs=in_vmem(1),
        out_specs=pl.BlockSpec(memory_space=pltpu.VMEM),
        compiler_params=params,
        name="joined",
    )(received)
    received = lax.all_to_all(copies, "seq", 0, 0, tiled=True)
    copies = pl.pallas_call(
        projected_kernel,
        out_shape=jax.ShapeDtypeStruct((heads, TOKENS, w_out.shape[1]), bf16),
        in_specs=[pl.BlockSpec(memory_space=pltpu.SMEM)] + in_vmem(4),
        out_specs=pl.BlockSpec(memory_space=pltpu.VMEM),
        compiler_params=params,
        name="projected",
    )(accepted, received, queries_draft, queries_verify, w_out)
    received = lax.all_to_all(copies, "tp", 0, 0, tiled=True)
    return pl.pallas_call(
        summed_kernel,
        out_shape=jax.ShapeDtypeStruct((ROUNDS, KINDS, BATCH * R, w_out.shape[1]), bf16),
        in_specs=in_vmem(1),
        out_specs=pl.BlockSpec(memory_space=pltpu.VMEM),
        compiler_params=params,
        name="summed",
    )(received)


def solution(mesh):
    in_specs = (
        P(None, None, "seq"),
        P("seq", "tp", None),
        P("tp", "seq"),
        P(None, None, "tp", None, None),
        P(None, None, "tp", None, None),
        P(None, "tp", "seq", None),
        P(None, "tp", "seq", None),
        P(None, "tp", "seq", None),
        P(None, "tp", "seq", None),
        P(None, "tp", "seq"),
        P(None, "tp", "seq"),
        P(),
        P(),
    )
    return jax.shard_map(
        per_device,
        mesh=mesh,
        in_specs=in_specs,
        out_specs=P(None, None, None, "seq"),
        check_vma=False,
    )
```

```python
import math

import jax
import jax.numpy as jnp
from jax import lax
from jax.experimental import pallas as pl
from jax.experimental.pallas import tpu as pltpu
from jax.sharding import PartitionSpec as P

HD = 128
GROUP = 8
R = 4
ROUNDS = 3
BATCH = 4
KINDS = 2
NEG = -1e30
SCALE = 1.0 / math.sqrt(HD)
SCALE_2 = SCALE / math.log(2.0)
ROWS = ROUNDS * GROUP * R
SHARE = KINDS * ROUNDS * R
NEW = ROUNDS * R
TOKENS = KINDS * ROUNDS * BATCH * R
TAIL = SHARE
PIECE = 3
MESSAGE = SHARE + 8
STEP = 512
FEW = 256
VMEM_LIMIT = 48 * 1024 * 1024

f32 = jnp.float32
bf16 = jnp.bfloat16


def rounded(x):
    return x.astype(bf16).astype(f32)


def dot(a, b):
    return jnp.dot(a, b, preferred_element_type=f32)


def dot_rows(a, b):
    return lax.dot_general(a, b, (((1,), (1,)), ((), ())), preferred_element_type=f32)


def parted(x):
    high = rounded(x)
    middle = rounded(x - high)
    return high, middle, x - high - middle


def by_head():
    row = lax.broadcasted_iota(jnp.int32, (KINDS * ROWS, KINDS * ROWS), 0)
    column = lax.broadcasted_iota(jnp.int32, (KINDS * ROWS, KINDS * ROWS), 1)
    target = ((column >> 2) & 7) * SHARE + ((column >> 5) << 2) + (column & 3)
    return jnp.where(row == target, 1.0, 0.0).astype(bf16)


def stats_spread(maxima, totals, place):
    lane = lax.broadcasted_iota(jnp.int32, (1, 128), 1)
    part = sum(jnp.where(lane >= k * SHARE, 1, 0) for k in range(1, 5))
    spread = jnp.zeros((maxima.shape[0], 128), f32)
    for k, x in enumerate(parted(maxima) + parted(totals)[:2]):
        spread = jnp.where(part == k, x, spread)
    return jnp.where(lane - part * SHARE == place, spread, 0.0)


def stats_of(rows):
    turned = rows.T
    parts = [turned[k * SHARE : (k + 1) * SHARE] for k in range(5)]
    return parts[0] + (parts[1] + parts[2]), parts[3] + parts[4]


def tails_of(received):
    return received[:, TAIL - 8 :].astype(f32)[:, 8:]


def lanes_folded(x, op):
    folded = x[:, :128]
    for k in range(1, x.shape[1] // 128):
        folded = op(folded, x[:, k * 128 : (k + 1) * 128])
    return folded


def attend(queries, keys, values, usable, scores, positions):
    step = min(STEP, positions)
    steps = range(0, positions, step)
    highest = None
    for at in steps:
        part = dot_rows(queries, keys(at, step))
        if usable is not None:
            lane = lax.broadcasted_iota(jnp.int32, (1, step), 1) + at
            part = part + jnp.where(lane < usable, 0.0, NEG)
        scores[:, at : at + step] = part
        folded = lanes_folded(part, jnp.maximum)
        highest = folded if highest is None else jnp.maximum(highest, folded)
    highest = jnp.max(highest, axis=1, keepdims=True)
    total = jnp.zeros((queries.shape[0], 128), f32)
    weighted = jnp.zeros((queries.shape[0], KINDS * HD), f32)
    for at in steps:
        weights = jnp.exp2((scores[:, at : at + step] - highest) * SCALE_2).astype(bf16)
        total = total + lanes_folded(weights.astype(f32), jnp.add)
        weighted = weighted + dot(weights, values(at, step))
    return highest * SCALE, jnp.sum(total, axis=1, keepdims=True), weighted


def partials_kernel(
    lengths_hbm,
    hidden_hbm,
    w_kv_hbm,
    queries_draft_hbm,
    queries_verify_hbm,
    keys_hbm,
    values_hbm,
    key_levels_hbm,
    value_levels_hbm,
    key_scales_hbm,
    value_scales_hbm,
    message,
    lengths,
    hidden,
    w_kv,
    queries_draft,
    queries_verify,
    keys,
    values,
    key_levels,
    value_levels,
    key_scales,
    value_scales,
    scores,
    sums,
    stats,
    order,
    tails,
    small_sems,
    cache_sems,
):
    local_len = keys.shape[1]
    few = min(FEW, local_len)
    small = [
        pltpu.make_async_copy(source, target, small_sems.at[k])
        for k, (source, target) in enumerate(
            (
                (lengths_hbm, lengths),
                (queries_draft_hbm, queries_draft),
                (queries_verify_hbm, queries_verify),
                (key_scales_hbm, key_scales),
                (value_scales_hbm, value_scales),
                (hidden_hbm, hidden),
                (w_kv_hbm, w_kv),
            )
        )
    ]
    for copy in small:
        copy.start()
    small[0].wait()
    first = lax.axis_index("seq") * local_len

    def usable_of(b):
        return jnp.clip(lengths[b] - first, 0, local_len)

    def cache_copies(b, rows):
        at = pl.ds(0, rows)
        return [
            pltpu.make_async_copy(source.at[b, 0, at], target.at[b, at], cache_sems.at[b, k])
            for k, (source, target) in enumerate(
                (
                    (key_levels_hbm, key_levels),
                    (keys_hbm, keys),
                    (value_levels_hbm, value_levels),
                    (values_hbm, values),
                )
            )
        ]

    for b in range(BATCH):
        usable = usable_of(b)

        @pl.when(usable > few)
        def _():
            for copy in cache_copies(b, local_len):
                copy.start()

        @pl.when((usable > 0) & (usable <= few))
        def _():
            for copy in cache_copies(b, few):
                copy.start()

    order[...] = by_head()
    for copy in small[1:]:
        copy.wait()
    part = dot(hidden[...].reshape(ROUNDS * BATCH * R, hidden.shape[2]), w_kv[...])
    part = jnp.concatenate([part[:, :HD], part[:, HD:]], axis=0)
    row = lax.broadcasted_iota(jnp.int32, (GROUP * BATCH * 8, 2 * TOKENS // KINDS), 0)
    column = lax.broadcasted_iota(jnp.int32, (GROUP * BATCH * 8, 2 * TOKENS // KINDS), 1)
    source = (row >> 3) * PIECE + (row & 7) - 1
    high = part.astype(bf16)
    low = (part - high.astype(f32)).astype(bf16)
    to_high = ((row & 7) >= 1) & ((row & 7) <= PIECE) & (column == source)
    to_low = ((row & 7) > PIECE) & ((row & 7) <= 2 * PIECE) & (column == source - PIECE)
    tails[...] = (
        dot(jnp.where(to_high, 1.0, 0.0).astype(bf16), high)
        + dot(jnp.where(to_low, 1.0, 0.0).astype(bf16), low)
    ).reshape(tails.shape)

    row = lax.broadcasted_iota(jnp.int32, (KINDS * ROWS, 1), 0)
    place = ((row >> 5) << 2) + (row & 3)
    row = lax.broadcasted_iota(jnp.int32, (GROUP, KINDS * ROWS), 0)
    column = lax.broadcasted_iota(jnp.int32, (GROUP, KINDS * ROWS), 1)
    of_head = jnp.where(((column >> 2) & 7) == row, 1.0, 0.0).astype(bf16)
    first_row = lax.broadcasted_iota(jnp.int32, (GROUP, 8, 128), 1) == 0

    def sequence(b, _):
        usable = usable_of(b)

        def over(positions, masked):
            copies = cache_copies(b, positions)

            def both(levels, scales, plain, ready):
                columns = scales[b].T

                def rows(at, step):
                    if at == 0:
                        for copy in ready:
                            copy.wait()
                    low = [
                        (levels[b, k : k + 128].astype(f32) * columns[:, k // 128 : k // 128 + 1]).astype(bf16)
                        for k in range(at, at + step, 128)
                    ]
                    return jnp.concatenate([jnp.concatenate(low, axis=0), plain[b, at : at + step]], axis=1)

                return rows

            zeros = jnp.zeros((ROWS, HD), bf16)
            rows = jnp.concatenate(
                [
                    jnp.concatenate([queries_draft[:, b, 0].reshape(ROWS, HD), zeros], axis=1),
                    jnp.concatenate([zeros, queries_verify[:, b, 0].reshape(ROWS, HD)], axis=1),
                ],
                axis=0,
            )
            maxima, totals, weighted = attend(
                rows,
                both(key_levels, key_scales, keys, copies[:2]),
                both(value_levels, value_scales, values, copies[2:]),
                usable if masked else None,
                scores,
                positions,
            )
            sums[b, :ROWS] = weighted[:ROWS, :HD].astype(bf16)
            sums[b, ROWS:] = weighted[ROWS:, HD:].astype(bf16)
            stats[b] = stats_spread(maxima, totals, place).astype(bf16)

        @pl.when(usable == 0)
        def _():
            sums[b] = jnp.zeros((KINDS * ROWS, HD), bf16)
            none = jnp.zeros((KINDS * ROWS, 1), f32)
            stats[b] = stats_spread(none + NEG, none, place).astype(bf16)

        @pl.when((usable > 0) & (usable <= few))
        def _():
            over(few, True)

        @pl.when((usable > few) & (usable < local_len))
        def _():
            over(local_len, True)

        @pl.when(usable == local_len)
        def _():
            over(local_len, False)

        return 0

    lax.fori_loop(0, BATCH, sequence, 0)
    for b in range(BATCH):
        ordered = dot(order[...], sums[b]).reshape(GROUP, SHARE, HD)
        head_stats = dot(of_head, stats[b]).reshape(GROUP, 1, 128)
        tail = jnp.where(first_row, head_stats, tails[:, b])
        message[:, b] = jnp.concatenate([ordered, tail], axis=1).astype(bf16)


def partials(lengths, *arrays):
    local_len = arrays[4].shape[2]
    hidden, w_kv, queries = arrays[:3]
    blocks = local_len // 128
    return pl.pallas_call(
        partials_kernel,
        out_shape=jax.ShapeDtypeStruct((GROUP, BATCH, MESSAGE, HD), bf16),
        in_specs=[pl.BlockSpec(memory_space=pltpu.HBM)] * (1 + len(arrays)),
        out_specs=pl.BlockSpec(memory_space=pltpu.VMEM),
        scratch_shapes=[
            pltpu.SMEM((BATCH,), jnp.int32),
            pltpu.VMEM(hidden.shape, bf16),
            pltpu.VMEM(w_kv.shape, bf16),
            pltpu.VMEM(queries.shape, bf16),
            pltpu.VMEM(queries.shape, bf16),
            pltpu.VMEM((BATCH, local_len, HD), bf16),
            pltpu.VMEM((BATCH, local_len, HD), bf16),
            pltpu.VMEM((BATCH, local_len, HD), bf16),
            pltpu.VMEM((BATCH, local_len, HD), bf16),
            pltpu.VMEM((BATCH, blocks, 128), f32),
            pltpu.VMEM((BATCH, blocks, 128), f32),
            pltpu.VMEM((KINDS * ROWS, local_len), f32),
            pltpu.VMEM((BATCH, KINDS * ROWS, HD), bf16),
            pltpu.VMEM((BATCH, KINDS * ROWS, 128), bf16),
            pltpu.VMEM((KINDS * ROWS, KINDS * ROWS), bf16),
            pltpu.VMEM((GROUP, BATCH, 8, 128), f32),
            pltpu.SemaphoreType.DMA((7,)),
            pltpu.SemaphoreType.DMA((BATCH, 4)),
        ],
        compiler_params=pltpu.CompilerParams(vmem_limit_bytes=VMEM_LIMIT),
        name="partials",
    )(*(pltpu.with_memory_space_constraint(x, pltpu.HBM) for x in (lengths, *arrays)))


def joined_kernel(received, copies):
    peers = received.shape[0]
    tails = tails_of(received)
    maxima, totals = stats_of(tails[:, 0])
    highest = jnp.max(maxima, axis=1, keepdims=True)
    factors = jnp.exp(maxima - highest)
    total = jnp.sum(totals * factors, axis=1, keepdims=True)
    sums = jnp.zeros((SHARE, HD), f32)
    for s in range(peers):
        sums = sums + factors[:, s : s + 1] * received[s].astype(f32)[:SHARE]
    fresh = jnp.sum(tails, axis=0)
    fresh = fresh + jnp.concatenate([fresh[PIECE:], fresh[:PIECE]], axis=0)
    place = lax.broadcasted_iota(jnp.int32, (SHARE, 1), 0)
    stats = jnp.sum(stats_spread(highest, total, place), axis=0, keepdims=True)
    row = lax.broadcasted_iota(jnp.int32, (8, 128), 0)
    tail = jnp.where(row == 0, stats, jnp.where(row <= PIECE, fresh, 0.0))
    block = jnp.concatenate([sums / total, tail], axis=0).astype(bf16)
    for s in range(peers):
        copies[s] = block


def projected_kernel(accepted, received, queries_draft, queries_verify, w_out, copies):
    peers = received.shape[0]
    tails = tails_of(received)
    row = lax.broadcasted_iota(jnp.int32, (BATCH * 2 * 16, peers * 8), 0)
    column = lax.broadcasted_iota(jnp.int32, (BATCH * 2 * 16, peers * 8), 1)
    within = (column & 7) - 1
    source = (column >> 3) * PIECE + within
    kv = jnp.where(source >= TOKENS // KINDS, 1, 0)
    token = source - kv * (TOKENS // KINDS)
    target = ((token >> 2) & 3) * 32 + kv * 16 + ((token >> 4) << 2) + (token & 3)
    chosen = (within >= 0) & (within < PIECE) & (row == target)
    fresh = dot(
        jnp.where(chosen, 1.0, 0.0).astype(bf16), tails.reshape(peers * 8, 128).astype(bf16)
    ).astype(bf16)

    maxima, totals = stats_of(tails[:, 0])
    order = by_head()
    row = lax.broadcasted_iota(jnp.int32, (KINDS * ROWS, 16), 0)
    column = lax.broadcasted_iota(jnp.int32, (KINDS * ROWS, 16), 1)
    turn = (row - ((row * 171) >> 12) * SHARE) >> 2
    turn = jnp.where(turn >= ROUNDS, turn - ROUNDS, turn)
    written, token = column >> 2, column & 3
    itself = (written == turn) & (token <= (row & 3))
    earlier = written < turn
    parts = []
    for b in range(BATCH):
        groups = [q[t, b, 0] for q in (queries_draft, queries_verify) for t in range(ROUNDS)]
        queries = dot(order, jnp.concatenate(groups, axis=0)).astype(bf16)
        kept = jnp.where(written == 0, accepted[0, b], jnp.where(written == 1, accepted[1, b], 0))
        visible = itself | (earlier & (token < kept))
        scores = jnp.where(visible, dot_rows(queries, fresh[b * 32 : b * 32 + 16]) * SCALE, NEG)
        new_highest = jnp.max(scores, axis=1, keepdims=True)
        weights = jnp.where(visible, jnp.exp(scores - new_highest), 0.0).astype(bf16)
        new_total = jnp.sum(weights.astype(f32), axis=1, keepdims=True)
        new_sums = dot(weights, fresh[b * 32 + 16 : b * 32 + 32])
        of_b = range(b, peers, BATCH)
        highest = jnp.concatenate([maxima[:, p : p + 1] for p in of_b], axis=0)
        total = jnp.concatenate([totals[:, p : p + 1] for p in of_b], axis=0)
        means = jnp.concatenate([received[p].astype(f32)[:SHARE] for p in of_b], axis=0)
        overall = jnp.maximum(highest, new_highest)
        factor = total * jnp.exp(highest - overall)
        new_factor = jnp.exp(new_highest - overall)
        whole = factor + new_total * new_factor
        attended = means * (factor / whole) + new_sums * (new_factor / whole)
        parts.append(
            jnp.concatenate([attended[g * SHARE : (g + 1) * SHARE] for g in range(GROUP)], axis=1)
        )
    out = dot(jnp.concatenate(parts, axis=0).astype(bf16), w_out[...]).astype(bf16)
    for k in range(copies.shape[0]):
        copies[k] = out


def summed_kernel(received, out):
    total = received[0].astype(f32)
    for k in range(1, received.shape[0]):
        total = total + received[k].astype(f32)
    row = lax.broadcasted_iota(jnp.int32, (TOKENS, TOKENS), 0)
    column = lax.broadcasted_iota(jnp.int32, (TOKENS, TOKENS), 1)
    at = row >> 2
    t, kind, b = at >> 3, (at >> 2) & 1, at & 3
    source = (b * KINDS * ROUNDS + kind * ROUNDS + t) * R + (row & 3)
    order = jnp.where(column == source, 1.0, 0.0).astype(bf16)
    ordered = dot(order, total.astype(bf16)).astype(bf16)
    out[...] = ordered.reshape(out.shape)


def in_vmem(count):
    return [pl.BlockSpec(memory_space=pltpu.VMEM)] * count


def per_device(
    hidden_new,
    w_kv,
    w_out,
    queries_draft,
    queries_verify,
    keys_cache,
    values_cache,
    key_levels,
    value_levels,
    key_scales,
    value_scales,
    lengths,
    accepted,
):
    peers, heads = lax.axis_size("seq"), lax.axis_size("tp")
    params = pltpu.CompilerParams(vmem_limit_bytes=VMEM_LIMIT)
    scales = [x.reshape(BATCH, -1, 128) for x in (key_scales, value_scales)]
    message = partials(
        lengths,
        hidden_new,
        w_kv.reshape(w_kv.shape[0], -1),
        queries_draft,
        queries_verify,
        keys_cache,
        values_cache,
        key_levels,
        value_levels,
        *scales,
    ).reshape(peers, MESSAGE, HD)
    received = lax.all_to_all(message, "seq", 0, 0, tiled=True)
    copies = pl.pallas_call(
        joined_kernel,
        out_shape=jax.ShapeDtypeStruct((peers, MESSAGE, HD), bf16),
        in_specs=in_vmem(1),
        out_specs=pl.BlockSpec(memory_space=pltpu.VMEM),
        compiler_params=params,
        name="joined",
    )(received)
    received = lax.all_to_all(copies, "seq", 0, 0, tiled=True)
    copies = pl.pallas_call(
        projected_kernel,
        out_shape=jax.ShapeDtypeStruct((heads, TOKENS, w_out.shape[1]), bf16),
        in_specs=[pl.BlockSpec(memory_space=pltpu.SMEM)] + in_vmem(4),
        out_specs=pl.BlockSpec(memory_space=pltpu.VMEM),
        compiler_params=params,
        name="projected",
    )(accepted, received, queries_draft, queries_verify, w_out)
    received = lax.all_to_all(copies, "tp", 0, 0, tiled=True)
    return pl.pallas_call(
        summed_kernel,
        out_shape=jax.ShapeDtypeStruct((ROUNDS, KINDS, BATCH * R, w_out.shape[1]), bf16),
        in_specs=in_vmem(1),
        out_specs=pl.BlockSpec(memory_space=pltpu.VMEM),
        compiler_params=params,
        name="summed",
    )(received)


def solution(mesh):
    in_specs = (
        P(None, None, "seq"),
        P("seq", "tp", None),
        P("tp", "seq"),
        P(None, None, "tp", None, None),
        P(None, None, "tp", None, None),
        P(None, "tp", "seq", None),
        P(None, "tp", "seq", None),
        P(None, "tp", "seq", None),
        P(None, "tp", "seq", None),
        P(None, "tp", "seq"),
        P(None, "tp", "seq"),
        P(),
        P(),
    )
    return jax.shard_map(
        per_device,
        mesh=mesh,
        in_specs=in_specs,
        out_specs=P(None, None, None, "seq"),
        check_vma=False,
    )
```

```python
import math

import jax
import jax.numpy as jnp
from jax import lax
from jax.experimental import pallas as pl
from jax.experimental.pallas import tpu as pltpu
from jax.sharding import PartitionSpec as P

HD = 128
GROUP = 8
R = 4
ROUNDS = 3
BATCH = 4
KINDS = 2
NEG = -1e30
SCALE = 1.0 / math.sqrt(HD)
SCALE_2 = SCALE / math.log(2.0)
ROWS = ROUNDS * GROUP * R
SHARE = KINDS * ROUNDS * R
NEW = ROUNDS * R
TOKENS = KINDS * ROUNDS * BATCH * R
TAIL = SHARE
PIECE = 3
MESSAGE = SHARE + 8
STEP = 512
FEW = 256
VMEM_LIMIT = 48 * 1024 * 1024

f32 = jnp.float32
bf16 = jnp.bfloat16


def rounded(x):
    return x.astype(bf16).astype(f32)


def dot(a, b):
    return jnp.dot(a, b, preferred_element_type=f32)


def dot_rows(a, b):
    return lax.dot_general(a, b, (((1,), (1,)), ((), ())), preferred_element_type=f32)


def parted(x):
    high = rounded(x)
    middle = rounded(x - high)
    return high, middle, x - high - middle


def by_head():
    row = lax.broadcasted_iota(jnp.int32, (KINDS * ROWS, KINDS * ROWS), 0)
    column = lax.broadcasted_iota(jnp.int32, (KINDS * ROWS, KINDS * ROWS), 1)
    target = ((column >> 2) & 7) * SHARE + ((column >> 5) << 2) + (column & 3)
    return jnp.where(row == target, 1.0, 0.0).astype(bf16)


def stats_spread(maxima, totals, place):
    lane = lax.broadcasted_iota(jnp.int32, (1, 128), 1)
    part = sum(jnp.where(lane >= k * SHARE, 1, 0) for k in range(1, 5))
    spread = jnp.zeros((maxima.shape[0], 128), f32)
    for k, x in enumerate(parted(maxima) + parted(totals)[:2]):
        spread = jnp.where(part == k, x, spread)
    return jnp.where(lane - part * SHARE == place, spread, 0.0)


def stats_of(rows):
    turned = rows.T
    parts = [turned[k * SHARE : (k + 1) * SHARE] for k in range(5)]
    return parts[0] + (parts[1] + parts[2]), parts[3] + parts[4]


def tails_of(received):
    return received[:, TAIL - 8 :].astype(f32)[:, 8:]


def lanes_folded(x, op):
    folded = x[:, :128]
    for k in range(1, x.shape[1] // 128):
        folded = op(folded, x[:, k * 128 : (k + 1) * 128])
    return folded


def attend(queries, keys, values, usable, scores, positions):
    step = min(STEP, positions)
    steps = range(0, positions, step)
    highest = None
    for at in steps:
        part = dot_rows(queries, keys(at, step))
        if usable is not None:
            lane = lax.broadcasted_iota(jnp.int32, (1, step), 1) + at
            part = part + jnp.where(lane < usable, 0.0, NEG)
        scores[:, at : at + step] = part
        folded = lanes_folded(part, jnp.maximum)
        highest = folded if highest is None else jnp.maximum(highest, folded)
    highest = jnp.max(highest, axis=1, keepdims=True)
    total = jnp.zeros((queries.shape[0], 128), f32)
    weighted = jnp.zeros((queries.shape[0], KINDS * HD), f32)
    for at in steps:
        weights = jnp.exp2((scores[:, at : at + step] - highest) * SCALE_2).astype(bf16)
        total = total + lanes_folded(weights.astype(f32), jnp.add)
        weighted = weighted + dot(weights, values(at, step))
    return highest * SCALE, jnp.sum(total, axis=1, keepdims=True), weighted


def partials_kernel(
    lengths_hbm,
    hidden_hbm,
    w_kv_hbm,
    queries_draft_hbm,
    queries_verify_hbm,
    keys_hbm,
    values_hbm,
    key_levels_hbm,
    value_levels_hbm,
    key_scales_hbm,
    value_scales_hbm,
    message,
    lengths,
    hidden,
    w_kv,
    queries_draft,
    queries_verify,
    keys,
    values,
    key_levels,
    value_levels,
    key_scales,
    value_scales,
    scores,
    sums,
    stats,
    order,
    tails,
    small_sems,
    cache_sems,
):
    local_len = keys.shape[1]
    few = min(FEW, local_len)
    small = [
        pltpu.make_async_copy(source, target, small_sems.at[k])
        for k, (source, target) in enumerate(
            (
                (lengths_hbm, lengths),
                (queries_draft_hbm, queries_draft),
                (queries_verify_hbm, queries_verify),
                (key_scales_hbm, key_scales),
                (value_scales_hbm, value_scales),
                (hidden_hbm, hidden),
                (w_kv_hbm, w_kv),
            )
        )
    ]
    for copy in small:
        copy.start()
    small[0].wait()
    first = lax.axis_index("seq") * local_len

    def usable_of(b):
        return jnp.clip(lengths[b] - first, 0, local_len)

    def cache_copies(b, rows):
        at = pl.ds(0, rows)
        return [
            pltpu.make_async_copy(source.at[b, 0, at], target.at[b, at], cache_sems.at[b, k])
            for k, (source, target) in enumerate(
                (
                    (key_levels_hbm, key_levels),
                    (keys_hbm, keys),
                    (value_levels_hbm, value_levels),
                    (values_hbm, values),
                )
            )
        ]

    for b in range(BATCH):
        usable = usable_of(b)

        @pl.when(usable > few)
        def _():
            for copy in cache_copies(b, local_len):
                copy.start()

        @pl.when((usable > 0) & (usable <= few))
        def _():
            for copy in cache_copies(b, few):
                copy.start()

    order[...] = by_head()
    for copy in small[1:]:
        copy.wait()
    part = dot(hidden[...].reshape(ROUNDS * BATCH * R, hidden.shape[2]), w_kv[...])
    part = jnp.concatenate([part[:, :HD], part[:, HD:]], axis=0)
    row = lax.broadcasted_iota(jnp.int32, (GROUP * BATCH * 8, 2 * TOKENS // KINDS), 0)
    column = lax.broadcasted_iota(jnp.int32, (GROUP * BATCH * 8, 2 * TOKENS // KINDS), 1)
    source = (row >> 3) * PIECE + (row & 7) - 1
    high = part.astype(bf16)
    low = (part - high.astype(f32)).astype(bf16)
    to_high = ((row & 7) >= 1) & ((row & 7) <= PIECE) & (column == source)
    to_low = ((row & 7) > PIECE) & ((row & 7) <= 2 * PIECE) & (column == source - PIECE)
    tails[...] = (
        dot(jnp.where(to_high, 1.0, 0.0).astype(bf16), high)
        + dot(jnp.where(to_low, 1.0, 0.0).astype(bf16), low)
    ).reshape(tails.shape)

    row = lax.broadcasted_iota(jnp.int32, (KINDS * ROWS, 1), 0)
    place = ((row >> 5) << 2) + (row & 3)
    row = lax.broadcasted_iota(jnp.int32, (GROUP, KINDS * ROWS), 0)
    column = lax.broadcasted_iota(jnp.int32, (GROUP, KINDS * ROWS), 1)
    of_head = jnp.where(((column >> 2) & 7) == row, 1.0, 0.0).astype(bf16)
    first_row = lax.broadcasted_iota(jnp.int32, (GROUP, 8, 128), 1) == 0

    def sequence(b, _):
        usable = usable_of(b)

        def over(positions, masked):
            copies = cache_copies(b, positions)

            def both(levels, scales, plain, ready):
                columns = scales[b].T

                def rows(at, step):
                    if at == 0:
                        for copy in ready:
                            copy.wait()
                    low = [
                        (levels[b, k : k + 128].astype(f32) * columns[:, k // 128 : k // 128 + 1]).astype(bf16)
                        for k in range(at, at + step, 128)
                    ]
                    return jnp.concatenate([jnp.concatenate(low, axis=0), plain[b, at : at + step]], axis=1)

                return rows

            zeros = jnp.zeros((ROWS, HD), bf16)
            rows = jnp.concatenate(
                [
                    jnp.concatenate([queries_draft[:, b, 0].reshape(ROWS, HD), zeros], axis=1),
                    jnp.concatenate([zeros, queries_verify[:, b, 0].reshape(ROWS, HD)], axis=1),
                ],
                axis=0,
            )
            maxima, totals, weighted = attend(
                rows,
                both(key_levels, key_scales, keys, copies[:2]),
                both(value_levels, value_scales, values, copies[2:]),
                usable if masked else None,
                scores,
                positions,
            )
            sums[b, :ROWS] = weighted[:ROWS, :HD].astype(bf16)
            sums[b, ROWS:] = weighted[ROWS:, HD:].astype(bf16)
            stats[b] = stats_spread(maxima, totals, place).astype(bf16)

        @pl.when(usable == 0)
        def _():
            sums[b] = jnp.zeros((KINDS * ROWS, HD), bf16)
            none = jnp.zeros((KINDS * ROWS, 1), f32)
            stats[b] = stats_spread(none + NEG, none, place).astype(bf16)

        @pl.when((usable > 0) & (usable <= few))
        def _():
            over(few, True)

        @pl.when((usable > few) & (usable < local_len))
        def _():
            over(local_len, True)

        @pl.when(usable == local_len)
        def _():
            over(local_len, False)

        return 0

    lax.fori_loop(0, BATCH, sequence, 0)
    for b in range(BATCH):
        ordered = dot(order[...], sums[b]).reshape(GROUP, SHARE, HD)
        head_stats = dot(of_head, stats[b]).reshape(GROUP, 1, 128)
        tail = jnp.where(first_row, head_stats, tails[:, b])
        message[:, b] = jnp.concatenate([ordered, tail], axis=1).astype(bf16)


def partials(lengths, *arrays):
    local_len = arrays[4].shape[2]
    hidden, w_kv, queries = arrays[:3]
    blocks = local_len // 128
    return pl.pallas_call(
        partials_kernel,
        out_shape=jax.ShapeDtypeStruct((GROUP, BATCH, MESSAGE, HD), bf16),
        in_specs=[pl.BlockSpec(memory_space=pltpu.HBM)] * (1 + len(arrays)),
        out_specs=pl.BlockSpec(memory_space=pltpu.VMEM),
        scratch_shapes=[
            pltpu.SMEM((BATCH,), jnp.int32),
            pltpu.VMEM(hidden.shape, bf16),
            pltpu.VMEM(w_kv.shape, bf16),
            pltpu.VMEM(queries.shape, bf16),
            pltpu.VMEM(queries.shape, bf16),
            pltpu.VMEM((BATCH, local_len, HD), bf16),
            pltpu.VMEM((BATCH, local_len, HD), bf16),
            pltpu.VMEM((BATCH, local_len, HD), bf16),
            pltpu.VMEM((BATCH, local_len, HD), bf16),
            pltpu.VMEM((BATCH, blocks, 128), f32),
            pltpu.VMEM((BATCH, blocks, 128), f32),
            pltpu.VMEM((KINDS * ROWS, local_len), f32),
            pltpu.VMEM((BATCH, KINDS * ROWS, HD), bf16),
            pltpu.VMEM((BATCH, KINDS * ROWS, 128), bf16),
            pltpu.VMEM((KINDS * ROWS, KINDS * ROWS), bf16),
            pltpu.VMEM((GROUP, BATCH, 8, 128), f32),
            pltpu.SemaphoreType.DMA((7,)),
            pltpu.SemaphoreType.DMA((BATCH, 4)),
        ],
        compiler_params=pltpu.CompilerParams(vmem_limit_bytes=VMEM_LIMIT),
        name="partials",
    )(*(pltpu.with_memory_space_constraint(x, pltpu.HBM) for x in (lengths, *arrays)))


def joined_kernel(received, copies):
    peers = received.shape[0]
    tails = tails_of(received)
    maxima, totals = stats_of(tails[:, 0])
    highest = jnp.max(maxima, axis=1, keepdims=True)
    factors = jnp.exp(maxima - highest)
    total = jnp.sum(totals * factors, axis=1, keepdims=True)
    sums = jnp.zeros((SHARE, HD), f32)
    for s in range(peers):
        sums = sums + factors[:, s : s + 1] * received[s].astype(f32)[:SHARE]
    fresh = jnp.sum(tails, axis=0)
    fresh = fresh + jnp.concatenate([fresh[PIECE:], fresh[:PIECE]], axis=0)
    place = lax.broadcasted_iota(jnp.int32, (SHARE, 1), 0)
    stats = jnp.sum(stats_spread(highest, total, place), axis=0, keepdims=True)
    row = lax.broadcasted_iota(jnp.int32, (8, 128), 0)
    tail = jnp.where(row == 0, stats, jnp.where(row <= PIECE, fresh, 0.0))
    block = jnp.concatenate([sums / total, tail], axis=0).astype(bf16)
    for s in range(peers):
        copies[s] = block


def prepared_kernel(_, accepted, queries_draft, queries_verify, queries, hidden, chosen, gather):
    order = by_head()
    row = lax.broadcasted_iota(jnp.int32, (KINDS * ROWS, 16), 0)
    column = lax.broadcasted_iota(jnp.int32, (KINDS * ROWS, 16), 1)
    turn = (row - ((row * 171) >> 12) * SHARE) >> 2
    turn = jnp.where(turn >= ROUNDS, turn - ROUNDS, turn)
    written, token = column >> 2, column & 3
    itself = (written == turn) & (token <= (row & 3))
    earlier = written < turn
    for b in range(BATCH):
        groups = [q[t, b, 0] for q in (queries_draft, queries_verify) for t in range(ROUNDS)]
        queries[b] = dot(order, jnp.concatenate(groups, axis=0)).astype(bf16)
        kept = jnp.where(written == 0, accepted[0, b], jnp.where(written == 1, accepted[1, b], 0))
        hidden[b] = jnp.where(itself | (earlier & (token < kept)), 0.0, NEG)
    row = lax.broadcasted_iota(jnp.int32, chosen.shape, 0)
    column = lax.broadcasted_iota(jnp.int32, chosen.shape, 1)
    within = (column & 7) - 1
    source = (column >> 3) * PIECE + within
    kv = jnp.where(source >= TOKENS // KINDS, 1, 0)
    token = source - kv * (TOKENS // KINDS)
    target = ((token >> 2) & 3) * 32 + kv * 16 + ((token >> 4) << 2) + (token & 3)
    taken = (within >= 0) & (within < PIECE) & (row == target)
    chosen[...] = jnp.where(taken, 1.0, 0.0).astype(bf16)
    row = lax.broadcasted_iota(jnp.int32, gather.shape, 0)
    column = lax.broadcasted_iota(jnp.int32, gather.shape, 1)
    at = row >> 2
    t, kind, b = at >> 3, (at >> 2) & 1, at & 3
    source = (b * KINDS * ROUNDS + kind * ROUNDS + t) * R + (row & 3)
    gather[...] = jnp.where(column == source, 1.0, 0.0).astype(bf16)


def projected_kernel(received, queries, hidden, chosen, w_out, copies):
    peers = received.shape[0]
    tails = tails_of(received)
    fresh = dot(chosen[...], tails.reshape(peers * 8, 128).astype(bf16)).astype(bf16)
    maxima, totals = stats_of(tails[:, 0])
    parts = []
    for b in range(BATCH):
        masked = hidden[b]
        scores = dot_rows(queries[b], fresh[b * 32 : b * 32 + 16]) * SCALE
        scores = jnp.where(masked == 0.0, scores, NEG)
        new_highest = jnp.max(scores, axis=1, keepdims=True)
        weights = jnp.exp(scores - new_highest).astype(bf16)
        new_total = jnp.sum(weights.astype(f32), axis=1, keepdims=True)
        new_sums = dot(weights, fresh[b * 32 + 16 : b * 32 + 32])
        of_b = range(b, peers, BATCH)
        highest = jnp.concatenate([maxima[:, p : p + 1] for p in of_b], axis=0)
        total = jnp.concatenate([totals[:, p : p + 1] for p in of_b], axis=0)
        means = jnp.concatenate([received[p].astype(f32)[:SHARE] for p in of_b], axis=0)
        overall = jnp.maximum(highest, new_highest)
        factor = total * jnp.exp(highest - overall)
        new_factor = jnp.exp(new_highest - overall)
        whole = factor + new_total * new_factor
        attended = means * (factor / whole) + new_sums * (new_factor / whole)
        parts.append(
            jnp.concatenate([attended[g * SHARE : (g + 1) * SHARE] for g in range(GROUP)], axis=1)
        )
    out = dot(jnp.concatenate(parts, axis=0).astype(bf16), w_out[...]).astype(bf16)
    for k in range(copies.shape[0]):
        copies[k] = out


def summed_kernel(received, gather, out):
    total = received[0].astype(f32)
    for k in range(1, received.shape[0]):
        total = total + received[k].astype(f32)
    ordered = dot(gather[...], total.astype(bf16)).astype(bf16)
    out[...] = ordered.reshape(out.shape)


def in_vmem(count):
    return [pl.BlockSpec(memory_space=pltpu.VMEM)] * count


def per_device(
    hidden_new,
    w_kv,
    w_out,
    queries_draft,
    queries_verify,
    keys_cache,
    values_cache,
    key_levels,
    value_levels,
    key_scales,
    value_scales,
    lengths,
    accepted,
):
    peers, heads = lax.axis_size("seq"), lax.axis_size("tp")
    params = pltpu.CompilerParams(vmem_limit_bytes=VMEM_LIMIT)
    scales = [x.reshape(BATCH, -1, 128) for x in (key_scales, value_scales)]
    message = partials(
        lengths,
        hidden_new,
        w_kv.reshape(w_kv.shape[0], -1),
        queries_draft,
        queries_verify,
        keys_cache,
        values_cache,
        key_levels,
        value_levels,
        *scales,
    ).reshape(peers, MESSAGE, HD)
    received = lax.all_to_all(message, "seq", 0, 0, tiled=True)
    shapes = (
        ((BATCH, KINDS * ROWS, HD), bf16),
        ((BATCH, KINDS * ROWS, 16), f32),
        ((BATCH * 2 * 16, peers * 8), bf16),
        ((TOKENS, TOKENS), bf16),
    )
    queries, hidden, chosen, gather = pl.pallas_call(
        prepared_kernel,
        out_shape=[jax.ShapeDtypeStruct(*shape) for shape in shapes],
        in_specs=[pl.BlockSpec(memory_space=pl.ANY), pl.BlockSpec(memory_space=pltpu.SMEM)] + in_vmem(2),
        out_specs=in_vmem(len(shapes)),
        compiler_params=params,
        cost_estimate=pl.CostEstimate(flops=40_000_000, bytes_accessed=4_000_000, transcendentals=0),
        name="prepared",
    )(message, accepted, queries_draft, queries_verify)
    copies = pl.pallas_call(
        joined_kernel,
        out_shape=jax.ShapeDtypeStruct((peers, MESSAGE, HD), bf16),
        in_specs=in_vmem(1),
        out_specs=pl.BlockSpec(memory_space=pltpu.VMEM),
        compiler_params=params,
        name="joined",
    )(received)
    received = lax.all_to_all(copies, "seq", 0, 0, tiled=True)
    copies = pl.pallas_call(
        projected_kernel,
        out_shape=jax.ShapeDtypeStruct((heads, TOKENS, w_out.shape[1]), bf16),
        in_specs=in_vmem(5),
        out_specs=pl.BlockSpec(memory_space=pltpu.VMEM),
        compiler_params=params,
        name="projected",
    )(received, queries, hidden, chosen, w_out)
    received = lax.all_to_all(copies, "tp", 0, 0, tiled=True)
    return pl.pallas_call(
        summed_kernel,
        out_shape=jax.ShapeDtypeStruct((ROUNDS, KINDS, BATCH * R, w_out.shape[1]), bf16),
        in_specs=in_vmem(2),
        out_specs=pl.BlockSpec(memory_space=pltpu.VMEM),
        compiler_params=params,
        name="summed",
    )(received, gather)


def solution(mesh):
    in_specs = (
        P(None, None, "seq"),
        P("seq", "tp", None),
        P("tp", "seq"),
        P(None, None, "tp", None, None),
        P(None, None, "tp", None, None),
        P(None, "tp", "seq", None),
        P(None, "tp", "seq", None),
        P(None, "tp", "seq", None),
        P(None, "tp", "seq", None),
        P(None, "tp", "seq"),
        P(None, "tp", "seq"),
        P(),
        P(),
    )
    return jax.shard_map(
        per_device,
        mesh=mesh,
        in_specs=in_specs,
        out_specs=P(None, None, None, "seq"),
        check_vma=False,
    )
```

```python
import math

import jax
import jax.numpy as jnp
from jax import lax
from jax.experimental import pallas as pl
from jax.experimental.pallas import tpu as pltpu
from jax.sharding import PartitionSpec as P

HD = 128
GROUP = 8
R = 4
ROUNDS = 3
BATCH = 4
KINDS = 2
NEG = -1e30
SCALE = 1.0 / math.sqrt(HD)
SCALE_2 = SCALE / math.log(2.0)
ROWS = ROUNDS * GROUP * R
SHARE = KINDS * ROUNDS * R
NEW = ROUNDS * R
TOKENS = KINDS * ROUNDS * BATCH * R
TAIL = SHARE
PIECE = 3
MESSAGE = SHARE + 8
CHOSEN = (BATCH * 2 * 16, GROUP * BATCH * 8)
STEP = 512
FEW = 256
VMEM_LIMIT = 48 * 1024 * 1024

f32 = jnp.float32
bf16 = jnp.bfloat16


def rounded(x):
    return x.astype(bf16).astype(f32)


def dot(a, b):
    return jnp.dot(a, b, preferred_element_type=f32)


def dot_rows(a, b):
    return lax.dot_general(a, b, (((1,), (1,)), ((), ())), preferred_element_type=f32)


def parted(x):
    high = rounded(x)
    middle = rounded(x - high)
    return high, middle, x - high - middle


def by_head():
    row = lax.broadcasted_iota(jnp.int32, (KINDS * ROWS, KINDS * ROWS), 0)
    column = lax.broadcasted_iota(jnp.int32, (KINDS * ROWS, KINDS * ROWS), 1)
    target = ((column >> 2) & 7) * SHARE + ((column >> 5) << 2) + (column & 3)
    return jnp.where(row == target, 1.0, 0.0).astype(bf16)


def fresh_selection():
    row = lax.broadcasted_iota(jnp.int32, CHOSEN, 0)
    column = lax.broadcasted_iota(jnp.int32, CHOSEN, 1)
    within = (column & 7) - 1
    source = (column >> 3) * PIECE + within
    kv = jnp.where(source >= TOKENS // KINDS, 1, 0)
    token = source - kv * (TOKENS // KINDS)
    target = ((token >> 2) & 3) * 32 + kv * 16 + ((token >> 4) << 2) + (token & 3)
    taken = (within >= 0) & (within < PIECE) & (row == target)
    return jnp.where(taken, 1.0, 0.0).astype(bf16)


def token_order():
    row = lax.broadcasted_iota(jnp.int32, (TOKENS, TOKENS), 0)
    column = lax.broadcasted_iota(jnp.int32, (TOKENS, TOKENS), 1)
    at = row >> 2
    t, kind, b = at >> 3, (at >> 2) & 1, at & 3
    source = (b * KINDS * ROUNDS + kind * ROUNDS + t) * R + (row & 3)
    return jnp.where(column == source, 1.0, 0.0).astype(bf16)


def stats_spread(maxima, totals, place):
    lane = lax.broadcasted_iota(jnp.int32, (1, 128), 1)
    part = sum(jnp.where(lane >= k * SHARE, 1, 0) for k in range(1, 5))
    spread = jnp.zeros((maxima.shape[0], 128), f32)
    for k, x in enumerate(parted(maxima) + parted(totals)[:2]):
        spread = jnp.where(part == k, x, spread)
    return jnp.where(lane - part * SHARE == place, spread, 0.0)


def stats_of(rows):
    turned = rows.T
    parts = [turned[k * SHARE : (k + 1) * SHARE] for k in range(5)]
    return parts[0] + (parts[1] + parts[2]), parts[3] + parts[4]


def tails_of(received):
    return received[:, TAIL - 8 :].astype(f32)[:, 8:]


def lanes_folded(x, op):
    folded = x[:, :128]
    for k in range(1, x.shape[1] // 128):
        folded = op(folded, x[:, k * 128 : (k + 1) * 128])
    return folded


def attend(queries, keys, values, usable, scores, positions):
    step = min(STEP, positions)
    steps = range(0, positions, step)
    highest = None
    for at in steps:
        part = dot_rows(queries, keys(at, step))
        if usable is not None:
            lane = lax.broadcasted_iota(jnp.int32, (1, step), 1) + at
            part = part + jnp.where(lane < usable, 0.0, NEG)
        scores[:, at : at + step] = part
        folded = lanes_folded(part, jnp.maximum)
        highest = folded if highest is None else jnp.maximum(highest, folded)
    highest = jnp.max(highest, axis=1, keepdims=True)
    total = jnp.zeros((queries.shape[0], 128), f32)
    weighted = jnp.zeros((queries.shape[0], KINDS * HD), f32)
    for at in steps:
        weights = jnp.exp2((scores[:, at : at + step] - highest) * SCALE_2).astype(bf16)
        total = total + lanes_folded(weights.astype(f32), jnp.add)
        weighted = weighted + dot(weights, values(at, step))
    return highest * SCALE, jnp.sum(total, axis=1, keepdims=True), weighted


def partials_kernel(
    lengths_hbm,
    accepted_hbm,
    hidden_hbm,
    w_kv_hbm,
    queries_draft_hbm,
    queries_verify_hbm,
    keys_hbm,
    values_hbm,
    key_levels_hbm,
    value_levels_hbm,
    key_scales_hbm,
    value_scales_hbm,
    message,
    by_head_queries,
    unseen,
    chosen,
    gather,
    lengths,
    accepted,
    hidden,
    w_kv,
    queries_draft,
    queries_verify,
    keys,
    values,
    key_levels,
    value_levels,
    key_scales,
    value_scales,
    scores,
    order,
    tails,
    small_sems,
    cache_sems,
):
    local_len = keys.shape[1]
    few = min(FEW, local_len)
    small = [
        pltpu.make_async_copy(source, target, small_sems.at[k])
        for k, (source, target) in enumerate(
            (
                (lengths_hbm, lengths),
                (accepted_hbm, accepted),
                (queries_draft_hbm, queries_draft),
                (queries_verify_hbm, queries_verify),
                (key_scales_hbm, key_scales),
                (value_scales_hbm, value_scales),
                (hidden_hbm, hidden),
                (w_kv_hbm, w_kv),
            )
        )
    ]
    for copy in small:
        copy.start()
    order[...] = by_head()
    chosen[...] = fresh_selection()
    gather[...] = token_order()
    small[0].wait()
    first = lax.axis_index("seq") * local_len

    def usable_of(b):
        return jnp.clip(lengths[b] - first, 0, local_len)

    def cache_copies(b, rows):
        at = pl.ds(0, rows)
        return [
            pltpu.make_async_copy(source.at[b, 0, at], target.at[b, at], cache_sems.at[b, k])
            for k, (source, target) in enumerate(
                (
                    (key_levels_hbm, key_levels),
                    (keys_hbm, keys),
                    (value_levels_hbm, value_levels),
                    (values_hbm, values),
                )
            )
        ]

    for b in range(BATCH):
        usable = usable_of(b)

        @pl.when(usable > few)
        def _():
            for copy in cache_copies(b, local_len):
                copy.start()

        @pl.when((usable > 0) & (usable <= few))
        def _():
            for copy in cache_copies(b, few):
                copy.start()

    for copy in small[1:]:
        copy.wait()
    part = dot(hidden[...].reshape(ROUNDS * BATCH * R, hidden.shape[2]), w_kv[...])
    part = jnp.concatenate([part[:, :HD], part[:, HD:]], axis=0)
    row = lax.broadcasted_iota(jnp.int32, (GROUP * BATCH * 8, 2 * TOKENS // KINDS), 0)
    column = lax.broadcasted_iota(jnp.int32, (GROUP * BATCH * 8, 2 * TOKENS // KINDS), 1)
    source = (row >> 3) * PIECE + (row & 7) - 1
    high = part.astype(bf16)
    low = (part - high.astype(f32)).astype(bf16)
    to_high = ((row & 7) >= 1) & ((row & 7) <= PIECE) & (column == source)
    to_low = ((row & 7) > PIECE) & ((row & 7) <= 2 * PIECE) & (column == source - PIECE)
    tails[...] = (
        dot(jnp.where(to_high, 1.0, 0.0).astype(bf16), high)
        + dot(jnp.where(to_low, 1.0, 0.0).astype(bf16), low)
    ).reshape(tails.shape)

    row = lax.broadcasted_iota(jnp.int32, (KINDS * ROWS, 1), 0)
    place = ((row >> 5) << 2) + (row & 3)
    row = lax.broadcasted_iota(jnp.int32, (GROUP, KINDS * ROWS), 0)
    column = lax.broadcasted_iota(jnp.int32, (GROUP, KINDS * ROWS), 1)
    of_head = jnp.where(((column >> 2) & 7) == row, 1.0, 0.0).astype(bf16)
    first_row = lax.broadcasted_iota(jnp.int32, (GROUP, 8, 128), 1) == 0

    row = lax.broadcasted_iota(jnp.int32, (KINDS * ROWS, 16), 0)
    column = lax.broadcasted_iota(jnp.int32, (KINDS * ROWS, 16), 1)
    turn = (row - ((row * 171) >> 12) * SHARE) >> 2
    turn = jnp.where(turn >= ROUNDS, turn - ROUNDS, turn)
    written, token = column >> 2, column & 3
    itself = (written == turn) & (token <= (row & 3))
    earlier = written < turn
    none = jnp.where(lax.broadcasted_iota(jnp.int32, (GROUP, 8, 128), 2) < SHARE, NEG, 0.0)
    for b in range(BATCH):
        groups = [q[t, b, 0] for q in (queries_draft, queries_verify) for t in range(ROUNDS)]
        by_head_queries[b] = dot(order[...], jnp.concatenate(groups, axis=0)).astype(bf16)
        kept = jnp.where(written == 0, accepted[0, b], jnp.where(written == 1, accepted[1, b], 0))
        unseen[b] = jnp.where(itself | (earlier & (token < kept)), 0.0, NEG)
        tail = jnp.where(first_row, none, tails[:, b])
        message[:, b] = jnp.concatenate([jnp.zeros((GROUP, SHARE, HD), f32), tail], axis=1).astype(bf16)

    def sequence(b, _):
        usable = usable_of(b)

        def over(positions, masked):
            copies = cache_copies(b, positions)

            def both(levels, scales, plain, ready):
                columns = scales[b].T

                def rows(at, step):
                    if at == 0:
                        for copy in ready:
                            copy.wait()
                    low = [
                        (levels[b, k : k + 128].astype(f32) * columns[:, k // 128 : k // 128 + 1]).astype(bf16)
                        for k in range(at, at + step, 128)
                    ]
                    return jnp.concatenate([jnp.concatenate(low, axis=0), plain[b, at : at + step]], axis=1)

                return rows

            zeros = jnp.zeros((ROWS, HD), bf16)
            rows = jnp.concatenate(
                [
                    jnp.concatenate([queries_draft[:, b, 0].reshape(ROWS, HD), zeros], axis=1),
                    jnp.concatenate([zeros, queries_verify[:, b, 0].reshape(ROWS, HD)], axis=1),
                ],
                axis=0,
            )
            maxima, totals, weighted = attend(
                rows,
                both(key_levels, key_scales, keys, copies[:2]),
                both(value_levels, value_scales, values, copies[2:]),
                usable if masked else None,
                scores,
                positions,
            )
            sums = jnp.concatenate([weighted[:ROWS, :HD], weighted[ROWS:, HD:]], axis=0).astype(bf16)
            stats = stats_spread(maxima, totals, place).astype(bf16)
            ordered = dot(order[...], sums).reshape(GROUP, SHARE, HD)
            tail = jnp.where(first_row, dot(of_head, stats).reshape(GROUP, 1, 128), tails[:, b])
            message[:, b] = jnp.concatenate([ordered, tail], axis=1).astype(bf16)

        @pl.when((usable > 0) & (usable <= few))
        def _():
            over(few, True)

        @pl.when((usable > few) & (usable < local_len))
        def _():
            over(local_len, True)

        @pl.when(usable == local_len)
        def _():
            over(local_len, False)

        return 0

    lax.fori_loop(0, BATCH, sequence, 0)


def partials(lengths, accepted, *arrays):
    local_len = arrays[4].shape[2]
    hidden, w_kv, queries = arrays[:3]
    blocks = local_len // 128
    return pl.pallas_call(
        partials_kernel,
        out_shape=[
            jax.ShapeDtypeStruct((GROUP, BATCH, MESSAGE, HD), bf16),
            jax.ShapeDtypeStruct((BATCH, KINDS * ROWS, HD), bf16),
            jax.ShapeDtypeStruct((BATCH, KINDS * ROWS, 16), f32),
            jax.ShapeDtypeStruct(CHOSEN, bf16),
            jax.ShapeDtypeStruct((TOKENS, TOKENS), bf16),
        ],
        in_specs=[pl.BlockSpec(memory_space=pltpu.HBM)] * (2 + len(arrays)),
        out_specs=[pl.BlockSpec(memory_space=pltpu.VMEM)] * 5,
        scratch_shapes=[
            pltpu.SMEM((BATCH,), jnp.int32),
            pltpu.SMEM(accepted.shape, jnp.int32),
            pltpu.VMEM(hidden.shape, bf16),
            pltpu.VMEM(w_kv.shape, bf16),
            pltpu.VMEM(queries.shape, bf16),
            pltpu.VMEM(queries.shape, bf16),
            pltpu.VMEM((BATCH, local_len, HD), bf16),
            pltpu.VMEM((BATCH, local_len, HD), bf16),
            pltpu.VMEM((BATCH, local_len, HD), bf16),
            pltpu.VMEM((BATCH, local_len, HD), bf16),
            pltpu.VMEM((BATCH, blocks, 128), f32),
            pltpu.VMEM((BATCH, blocks, 128), f32),
            pltpu.VMEM((KINDS * ROWS, local_len), f32),
            pltpu.VMEM((KINDS * ROWS, KINDS * ROWS), bf16),
            pltpu.VMEM((GROUP, BATCH, 8, 128), f32),
            pltpu.SemaphoreType.DMA((8,)),
            pltpu.SemaphoreType.DMA((BATCH, 4)),
        ],
        compiler_params=pltpu.CompilerParams(vmem_limit_bytes=VMEM_LIMIT),
        name="partials",
    )(*(pltpu.with_memory_space_constraint(x, pltpu.HBM) for x in (lengths, accepted, *arrays)))


def joined_kernel(received, copies):
    peers = received.shape[0]
    tails = tails_of(received)
    maxima, totals = stats_of(tails[:, 0])
    highest = jnp.max(maxima, axis=1, keepdims=True)
    factors = jnp.exp(maxima - highest)
    total = jnp.sum(totals * factors, axis=1, keepdims=True)
    sums = jnp.zeros((SHARE, HD), f32)
    for s in range(peers):
        sums = sums + factors[:, s : s + 1] * received[s].astype(f32)[:SHARE]
    fresh = jnp.sum(tails, axis=0)
    fresh = fresh + jnp.concatenate([fresh[PIECE:], fresh[:PIECE]], axis=0)
    place = lax.broadcasted_iota(jnp.int32, (SHARE, 1), 0)
    stats = jnp.sum(stats_spread(highest, total, place), axis=0, keepdims=True)
    row = lax.broadcasted_iota(jnp.int32, (8, 128), 0)
    tail = jnp.where(row == 0, stats, jnp.where(row <= PIECE, fresh, 0.0))
    block = jnp.concatenate([sums / total, tail], axis=0).astype(bf16)
    for s in range(peers):
        copies[s] = block


def projected_kernel(received, queries, unseen, chosen, w_out, copies):
    peers = received.shape[0]
    tails = tails_of(received)
    fresh = dot(chosen[...], tails.reshape(peers * 8, 128).astype(bf16)).astype(bf16)
    maxima, totals = stats_of(tails[:, 0])
    parts = []
    for b in range(BATCH):
        scores = dot_rows(queries[b], fresh[b * 32 : b * 32 + 16]) * SCALE
        scores = jnp.where(unseen[b] == 0.0, scores, NEG)
        new_highest = jnp.max(scores, axis=1, keepdims=True)
        weights = jnp.exp(scores - new_highest).astype(bf16)
        new_total = jnp.sum(weights.astype(f32), axis=1, keepdims=True)
        new_sums = dot(weights, fresh[b * 32 + 16 : b * 32 + 32])
        of_b = range(b, peers, BATCH)
        highest = jnp.concatenate([maxima[:, p : p + 1] for p in of_b], axis=0)
        total = jnp.concatenate([totals[:, p : p + 1] for p in of_b], axis=0)
        means = jnp.concatenate([received[p].astype(f32)[:SHARE] for p in of_b], axis=0)
        overall = jnp.maximum(highest, new_highest)
        factor = total * jnp.exp(highest - overall)
        new_factor = jnp.exp(new_highest - overall)
        whole = factor + new_total * new_factor
        attended = means * (factor / whole) + new_sums * (new_factor / whole)
        parts.append(
            jnp.concatenate([attended[g * SHARE : (g + 1) * SHARE] for g in range(GROUP)], axis=1)
        )
    out = dot(jnp.concatenate(parts, axis=0).astype(bf16), w_out[...]).astype(bf16)
    for k in range(copies.shape[0]):
        copies[k] = out


def summed_kernel(received, gather, out):
    total = received[0].astype(f32)
    for k in range(1, received.shape[0]):
        total = total + received[k].astype(f32)
    ordered = dot(gather[...], total.astype(bf16)).astype(bf16)
    out[...] = ordered.reshape(out.shape)


def in_vmem(count):
    return [pl.BlockSpec(memory_space=pltpu.VMEM)] * count


def per_device(
    hidden_new,
    w_kv,
    w_out,
    queries_draft,
    queries_verify,
    keys_cache,
    values_cache,
    key_levels,
    value_levels,
    key_scales,
    value_scales,
    lengths,
    accepted,
):
    peers, heads = lax.axis_size("seq"), lax.axis_size("tp")
    params = pltpu.CompilerParams(vmem_limit_bytes=VMEM_LIMIT)
    scales = [x.reshape(BATCH, -1, 128) for x in (key_scales, value_scales)]
    message, queries, unseen, chosen, gather = partials(
        lengths,
        accepted,
        hidden_new,
        w_kv.reshape(w_kv.shape[0], -1),
        queries_draft,
        queries_verify,
        keys_cache,
        values_cache,
        key_levels,
        value_levels,
        *scales,
    )
    received = lax.all_to_all(message.reshape(peers, MESSAGE, HD), "seq", 0, 0, tiled=True)
    copies = pl.pallas_call(
        joined_kernel,
        out_shape=jax.ShapeDtypeStruct((peers, MESSAGE, HD), bf16),
        in_specs=in_vmem(1),
        out_specs=pl.BlockSpec(memory_space=pltpu.VMEM),
        compiler_params=params,
        name="joined",
    )(received)
    received = lax.all_to_all(copies, "seq", 0, 0, tiled=True)
    copies = pl.pallas_call(
        projected_kernel,
        out_shape=jax.ShapeDtypeStruct((heads, TOKENS, w_out.shape[1]), bf16),
        in_specs=in_vmem(5),
        out_specs=pl.BlockSpec(memory_space=pltpu.VMEM),
        compiler_params=params,
        name="projected",
    )(received, queries, unseen, chosen, w_out)
    received = lax.all_to_all(copies, "tp", 0, 0, tiled=True)
    return pl.pallas_call(
        summed_kernel,
        out_shape=jax.ShapeDtypeStruct((ROUNDS, KINDS, BATCH * R, w_out.shape[1]), bf16),
        in_specs=in_vmem(2),
        out_specs=pl.BlockSpec(memory_space=pltpu.VMEM),
        compiler_params=params,
        name="summed",
    )(received, gather)


def solution(mesh):
    in_specs = (
        P(None, None, "seq"),
        P("seq", "tp", None),
        P("tp", "seq"),
        P(None, None, "tp", None, None),
        P(None, None, "tp", None, None),
        P(None, "tp", "seq", None),
        P(None, "tp", "seq", None),
        P(None, "tp", "seq", None),
        P(None, "tp", "seq", None),
        P(None, "tp", "seq"),
        P(None, "tp", "seq"),
        P(),
        P(),
    )
    return jax.shard_map(
        per_device,
        mesh=mesh,
        in_specs=in_specs,
        out_specs=P(None, None, None, "seq"),
        check_vma=False,
    )
```

```python
import math

import jax
import jax.numpy as jnp
from jax import lax
from jax.experimental import pallas as pl
from jax.experimental.pallas import tpu as pltpu
from jax.sharding import PartitionSpec as P

HD = 128
GROUP = 8
R = 4
ROUNDS = 3
BATCH = 4
KINDS = 2
NEG = -1e30
SCALE = 1.0 / math.sqrt(HD)
SCALE_2 = SCALE / math.log(2.0)
ROWS = ROUNDS * GROUP * R
SHARE = KINDS * ROUNDS * R
NEW = ROUNDS * R
TOKENS = KINDS * ROUNDS * BATCH * R
TAIL = SHARE
PIECE = 3
MESSAGE = SHARE + 8
CHOSEN = (BATCH * 2 * 16, GROUP * BATCH * 8)
STEP = 512
FEW = 256
VMEM_LIMIT = 48 * 1024 * 1024

f32 = jnp.float32
bf16 = jnp.bfloat16


def rounded(x):
    return x.astype(bf16).astype(f32)


def dot(a, b):
    return jnp.dot(a, b, preferred_element_type=f32)


def dot_rows(a, b):
    return lax.dot_general(a, b, (((1,), (1,)), ((), ())), preferred_element_type=f32)


def parted(x):
    high = rounded(x)
    middle = rounded(x - high)
    return high, middle, x - high - middle


def by_head():
    row = lax.broadcasted_iota(jnp.int32, (KINDS * ROWS, KINDS * ROWS), 0)
    column = lax.broadcasted_iota(jnp.int32, (KINDS * ROWS, KINDS * ROWS), 1)
    target = ((column >> 2) & 7) * SHARE + ((column >> 5) << 2) + (column & 3)
    return jnp.where(row == target, 1.0, 0.0).astype(bf16)


def fresh_selection():
    row = lax.broadcasted_iota(jnp.int32, CHOSEN, 0)
    column = lax.broadcasted_iota(jnp.int32, CHOSEN, 1)
    within = (column & 7) - 1
    source = (column >> 3) * PIECE + within
    kv = jnp.where(source >= TOKENS // KINDS, 1, 0)
    token = source - kv * (TOKENS // KINDS)
    target = ((token >> 2) & 3) * 32 + kv * 16 + ((token >> 4) << 2) + (token & 3)
    taken = (within >= 0) & (within < PIECE) & (row == target)
    return jnp.where(taken, 1.0, 0.0).astype(bf16)


def token_order(shares):
    row = lax.broadcasted_iota(jnp.int32, (TOKENS, shares * TOKENS), 0)
    column = lax.broadcasted_iota(jnp.int32, (1, shares * TOKENS), 1)
    column = column - TOKENS * sum(jnp.where(column >= k * TOKENS, 1, 0) for k in range(1, shares))
    at = row >> 2
    t, kind, b = at >> 3, (at >> 2) & 1, at & 3
    source = (b * KINDS * ROUNDS + kind * ROUNDS + t) * R + (row & 3)
    return jnp.where(column == source, 1.0, 0.0).astype(bf16)


def stats_spread(maxima, totals, place):
    lane = lax.broadcasted_iota(jnp.int32, (1, 128), 1)
    part = sum(jnp.where(lane >= k * SHARE, 1, 0) for k in range(1, 5))
    spread = jnp.zeros((maxima.shape[0], 128), f32)
    for k, x in enumerate(parted(maxima) + parted(totals)[:2]):
        spread = jnp.where(part == k, x, spread)
    return jnp.where(lane - part * SHARE == place, spread, 0.0)


def stats_of(rows):
    turned = rows.T
    parts = [turned[k * SHARE : (k + 1) * SHARE] for k in range(5)]
    return parts[0] + (parts[1] + parts[2]), parts[3] + parts[4]


def tails_of(received):
    return received[:, TAIL - 8 :].astype(f32)[:, 8:]


def lanes_folded(x, op):
    folded = x[:, :128]
    for k in range(1, x.shape[1] // 128):
        folded = op(folded, x[:, k * 128 : (k + 1) * 128])
    return folded


def attend(queries, keys, values, usable, scores, positions):
    step = min(STEP, positions)
    steps = range(0, positions, step)
    highest = None
    for at in steps:
        part = dot_rows(queries, keys(at, step))
        if usable is not None:
            lane = lax.broadcasted_iota(jnp.int32, (1, step), 1) + at
            part = part + jnp.where(lane < usable, 0.0, NEG)
        scores[:, at : at + step] = part
        folded = lanes_folded(part, jnp.maximum)
        highest = folded if highest is None else jnp.maximum(highest, folded)
    highest = jnp.max(highest, axis=1, keepdims=True)
    total = jnp.zeros((queries.shape[0], 128), f32)
    weighted = jnp.zeros((queries.shape[0], KINDS * HD), f32)
    for at in steps:
        weights = jnp.exp2((scores[:, at : at + step] - highest) * SCALE_2).astype(bf16)
        total = total + lanes_folded(weights.astype(f32), jnp.add)
        weighted = weighted + dot(weights, values(at, step))
    return highest * SCALE, jnp.sum(total, axis=1, keepdims=True), weighted


def partials_kernel(
    lengths_hbm,
    accepted_hbm,
    hidden_hbm,
    w_kv_hbm,
    queries_draft_hbm,
    queries_verify_hbm,
    keys_hbm,
    values_hbm,
    key_levels_hbm,
    value_levels_hbm,
    key_scales_hbm,
    value_scales_hbm,
    message,
    by_head_queries,
    unseen,
    chosen,
    gather,
    lengths,
    accepted,
    hidden,
    w_kv,
    queries_draft,
    queries_verify,
    keys,
    values,
    key_levels,
    value_levels,
    key_scales,
    value_scales,
    scores,
    order,
    tails,
    small_sems,
    cache_sems,
):
    local_len = keys.shape[1]
    few = min(FEW, local_len)
    small = [
        pltpu.make_async_copy(source, target, small_sems.at[k])
        for k, (source, target) in enumerate(
            (
                (lengths_hbm, lengths),
                (accepted_hbm, accepted),
                (queries_draft_hbm, queries_draft),
                (queries_verify_hbm, queries_verify),
                (key_scales_hbm, key_scales),
                (value_scales_hbm, value_scales),
                (hidden_hbm, hidden),
                (w_kv_hbm, w_kv),
            )
        )
    ]
    for copy in small:
        copy.start()
    order[...] = by_head()
    chosen[...] = fresh_selection()
    gather[...] = token_order(gather.shape[1] // TOKENS)
    small[0].wait()
    first = lax.axis_index("seq") * local_len

    def usable_of(b):
        return jnp.clip(lengths[b] - first, 0, local_len)

    def cache_copies(b, rows):
        at = pl.ds(0, rows)
        return [
            pltpu.make_async_copy(source.at[b, 0, at], target.at[b, at], cache_sems.at[b, k])
            for k, (source, target) in enumerate(
                (
                    (key_levels_hbm, key_levels),
                    (keys_hbm, keys),
                    (value_levels_hbm, value_levels),
                    (values_hbm, values),
                )
            )
        ]

    for b in range(BATCH):
        usable = usable_of(b)

        @pl.when(usable > few)
        def _():
            for copy in cache_copies(b, local_len):
                copy.start()

        @pl.when((usable > 0) & (usable <= few))
        def _():
            for copy in cache_copies(b, few):
                copy.start()

    for copy in small[1:]:
        copy.wait()
    part = dot(hidden[...].reshape(ROUNDS * BATCH * R, hidden.shape[2]), w_kv[...])
    part = jnp.concatenate([part[:, :HD], part[:, HD:]], axis=0)
    row = lax.broadcasted_iota(jnp.int32, (GROUP * BATCH * 8, 2 * TOKENS // KINDS), 0)
    column = lax.broadcasted_iota(jnp.int32, (GROUP * BATCH * 8, 2 * TOKENS // KINDS), 1)
    source = (row >> 3) * PIECE + (row & 7) - 1
    high = part.astype(bf16)
    low = (part - high.astype(f32)).astype(bf16)
    to_high = ((row & 7) >= 1) & ((row & 7) <= PIECE) & (column == source)
    to_low = ((row & 7) > PIECE) & ((row & 7) <= 2 * PIECE) & (column == source - PIECE)
    tails[...] = (
        dot(jnp.where(to_high, 1.0, 0.0).astype(bf16), high)
        + dot(jnp.where(to_low, 1.0, 0.0).astype(bf16), low)
    ).reshape(tails.shape)

    row = lax.broadcasted_iota(jnp.int32, (KINDS * ROWS, 1), 0)
    place = ((row >> 5) << 2) + (row & 3)
    row = lax.broadcasted_iota(jnp.int32, (GROUP, KINDS * ROWS), 0)
    column = lax.broadcasted_iota(jnp.int32, (GROUP, KINDS * ROWS), 1)
    of_head = jnp.where(((column >> 2) & 7) == row, 1.0, 0.0).astype(bf16)
    first_row = lax.broadcasted_iota(jnp.int32, (GROUP, 8, 128), 1) == 0

    row = lax.broadcasted_iota(jnp.int32, (KINDS * ROWS, 16), 0)
    column = lax.broadcasted_iota(jnp.int32, (KINDS * ROWS, 16), 1)
    turn = (row - ((row * 171) >> 12) * SHARE) >> 2
    turn = jnp.where(turn >= ROUNDS, turn - ROUNDS, turn)
    written, token = column >> 2, column & 3
    itself = (written == turn) & (token <= (row & 3))
    earlier = written < turn
    none = jnp.where(lax.broadcasted_iota(jnp.int32, (GROUP, 8, 128), 2) < SHARE, NEG, 0.0)
    for b in range(BATCH):
        groups = [q[t, b, 0] for q in (queries_draft, queries_verify) for t in range(ROUNDS)]
        by_head_queries[b] = dot(order[...], jnp.concatenate(groups, axis=0)).astype(bf16)
        kept = jnp.where(written == 0, accepted[0, b], jnp.where(written == 1, accepted[1, b], 0))
        unseen[b] = jnp.where(itself | (earlier & (token < kept)), 0.0, NEG)
        tail = jnp.where(first_row, none, tails[:, b])
        message[:, b] = jnp.concatenate([jnp.zeros((GROUP, SHARE, HD), f32), tail], axis=1).astype(bf16)

    def sequence(b, _):
        usable = usable_of(b)

        def over(positions, masked):
            copies = cache_copies(b, positions)

            def both(levels, scales, plain, ready):
                columns = scales[b].T

                def rows(at, step):
                    if at == 0:
                        for copy in ready:
                            copy.wait()
                    low = [
                        (levels[b, k : k + 128].astype(f32) * columns[:, k // 128 : k // 128 + 1]).astype(bf16)
                        for k in range(at, at + step, 128)
                    ]
                    return jnp.concatenate([jnp.concatenate(low, axis=0), plain[b, at : at + step]], axis=1)

                return rows

            zeros = jnp.zeros((ROWS, HD), bf16)
            rows = jnp.concatenate(
                [
                    jnp.concatenate([queries_draft[:, b, 0].reshape(ROWS, HD), zeros], axis=1),
                    jnp.concatenate([zeros, queries_verify[:, b, 0].reshape(ROWS, HD)], axis=1),
                ],
                axis=0,
            )
            maxima, totals, weighted = attend(
                rows,
                both(key_levels, key_scales, keys, copies[:2]),
                both(value_levels, value_scales, values, copies[2:]),
                usable if masked else None,
                scores,
                positions,
            )
            sums = jnp.concatenate([weighted[:ROWS, :HD], weighted[ROWS:, HD:]], axis=0).astype(bf16)
            stats = stats_spread(maxima, totals, place).astype(bf16)
            ordered = dot(order[...], sums).reshape(GROUP, SHARE, HD)
            tail = jnp.where(first_row, dot(of_head, stats).reshape(GROUP, 1, 128), tails[:, b])
            message[:, b] = jnp.concatenate([ordered, tail], axis=1).astype(bf16)

        @pl.when((usable > 0) & (usable <= few))
        def _():
            over(few, True)

        @pl.when((usable > few) & (usable < local_len))
        def _():
            over(local_len, True)

        @pl.when(usable == local_len)
        def _():
            over(local_len, False)

        return 0

    lax.fori_loop(0, BATCH, sequence, 0)


def partials(lengths, accepted, *arrays):
    local_len = arrays[4].shape[2]
    hidden, w_kv, queries = arrays[:3]
    blocks = local_len // 128
    return pl.pallas_call(
        partials_kernel,
        out_shape=[
            jax.ShapeDtypeStruct((GROUP, BATCH, MESSAGE, HD), bf16),
            jax.ShapeDtypeStruct((BATCH, KINDS * ROWS, HD), bf16),
            jax.ShapeDtypeStruct((BATCH, KINDS * ROWS, 16), f32),
            jax.ShapeDtypeStruct(CHOSEN, bf16),
            jax.ShapeDtypeStruct((TOKENS, lax.axis_size("tp") * TOKENS), bf16),
        ],
        in_specs=[pl.BlockSpec(memory_space=pltpu.HBM)] * (2 + len(arrays)),
        out_specs=[pl.BlockSpec(memory_space=pltpu.VMEM)] * 5,
        scratch_shapes=[
            pltpu.SMEM((BATCH,), jnp.int32),
            pltpu.SMEM(accepted.shape, jnp.int32),
            pltpu.VMEM(hidden.shape, bf16),
            pltpu.VMEM(w_kv.shape, bf16),
            pltpu.VMEM(queries.shape, bf16),
            pltpu.VMEM(queries.shape, bf16),
            pltpu.VMEM((BATCH, local_len, HD), bf16),
            pltpu.VMEM((BATCH, local_len, HD), bf16),
            pltpu.VMEM((BATCH, local_len, HD), bf16),
            pltpu.VMEM((BATCH, local_len, HD), bf16),
            pltpu.VMEM((BATCH, blocks, 128), f32),
            pltpu.VMEM((BATCH, blocks, 128), f32),
            pltpu.VMEM((KINDS * ROWS, local_len), f32),
            pltpu.VMEM((KINDS * ROWS, KINDS * ROWS), bf16),
            pltpu.VMEM((GROUP, BATCH, 8, 128), f32),
            pltpu.SemaphoreType.DMA((8,)),
            pltpu.SemaphoreType.DMA((BATCH, 4)),
        ],
        compiler_params=pltpu.CompilerParams(vmem_limit_bytes=VMEM_LIMIT),
        name="partials",
    )(*(pltpu.with_memory_space_constraint(x, pltpu.HBM) for x in (lengths, accepted, *arrays)))


def joined_kernel(received, copies):
    peers = received.shape[0]
    tails = tails_of(received)
    maxima, totals = stats_of(tails[:, 0])
    highest = jnp.max(maxima, axis=1, keepdims=True)
    factors = jnp.exp(maxima - highest)
    total = jnp.sum(totals * factors, axis=1, keepdims=True)
    sums = jnp.zeros((SHARE, HD), f32)
    for s in range(peers):
        sums = sums + factors[:, s : s + 1] * received[s].astype(f32)[:SHARE]
    fresh = jnp.sum(tails, axis=0)
    fresh = fresh + jnp.concatenate([fresh[PIECE:], fresh[:PIECE]], axis=0)
    place = lax.broadcasted_iota(jnp.int32, (SHARE, 1), 0)
    stats = jnp.sum(stats_spread(highest, total, place), axis=0, keepdims=True)
    row = lax.broadcasted_iota(jnp.int32, (8, 128), 0)
    tail = jnp.where(row == 0, stats, jnp.where(row <= PIECE, fresh, 0.0))
    block = jnp.concatenate([sums / total, tail], axis=0).astype(bf16)
    for s in range(peers):
        copies[s] = block


def projected_kernel(received, queries, unseen, chosen, w_out, copies):
    peers = received.shape[0]
    tails = tails_of(received)
    fresh = dot(chosen[...], tails.reshape(peers * 8, 128).astype(bf16)).astype(bf16)
    maxima, totals = stats_of(tails[:, 0])
    parts = []
    for b in range(BATCH):
        scores = dot_rows(queries[b], fresh[b * 32 : b * 32 + 16]) * SCALE
        scores = jnp.where(unseen[b] == 0.0, scores, NEG)
        new_highest = jnp.max(scores, axis=1, keepdims=True)
        weights = jnp.exp(scores - new_highest).astype(bf16)
        new_total = jnp.sum(weights.astype(f32), axis=1, keepdims=True)
        new_sums = dot(weights, fresh[b * 32 + 16 : b * 32 + 32])
        of_b = range(b, peers, BATCH)
        highest = jnp.concatenate([maxima[:, p : p + 1] for p in of_b], axis=0)
        total = jnp.concatenate([totals[:, p : p + 1] for p in of_b], axis=0)
        means = jnp.concatenate([received[p].astype(f32)[:SHARE] for p in of_b], axis=0)
        overall = jnp.maximum(highest, new_highest)
        factor = total * jnp.exp(highest - overall)
        new_factor = jnp.exp(new_highest - overall)
        whole = factor + new_total * new_factor
        attended = means * (factor / whole) + new_sums * (new_factor / whole)
        parts.append(
            jnp.concatenate([attended[g * SHARE : (g + 1) * SHARE] for g in range(GROUP)], axis=1)
        )
    out = dot(jnp.concatenate(parts, axis=0).astype(bf16), w_out[...]).astype(bf16)
    for k in range(copies.shape[0]):
        copies[k] = out


def summed_kernel(received, gather, out):
    shares = received[...].reshape(-1, received.shape[2])
    out[...] = dot(gather[...], shares).astype(bf16).reshape(out.shape)


def in_vmem(count):
    return [pl.BlockSpec(memory_space=pltpu.VMEM)] * count


def per_device(
    hidden_new,
    w_kv,
    w_out,
    queries_draft,
    queries_verify,
    keys_cache,
    values_cache,
    key_levels,
    value_levels,
    key_scales,
    value_scales,
    lengths,
    accepted,
):
    peers, heads = lax.axis_size("seq"), lax.axis_size("tp")
    params = pltpu.CompilerParams(vmem_limit_bytes=VMEM_LIMIT)
    scales = [x.reshape(BATCH, -1, 128) for x in (key_scales, value_scales)]
    message, queries, unseen, chosen, gather = partials(
        lengths,
        accepted,
        hidden_new,
        w_kv.reshape(w_kv.shape[0], -1),
        queries_draft,
        queries_verify,
        keys_cache,
        values_cache,
        key_levels,
        value_levels,
        *scales,
    )
    received = lax.all_to_all(message.reshape(peers, MESSAGE, HD), "seq", 0, 0, tiled=True)
    copies = pl.pallas_call(
        joined_kernel,
        out_shape=jax.ShapeDtypeStruct((peers, MESSAGE, HD), bf16),
        in_specs=in_vmem(1),
        out_specs=pl.BlockSpec(memory_space=pltpu.VMEM),
        compiler_params=params,
        name="joined",
    )(received)
    received = lax.all_to_all(copies, "seq", 0, 0, tiled=True)
    copies = pl.pallas_call(
        projected_kernel,
        out_shape=jax.ShapeDtypeStruct((heads, TOKENS, w_out.shape[1]), bf16),
        in_specs=in_vmem(5),
        out_specs=pl.BlockSpec(memory_space=pltpu.VMEM),
        compiler_params=params,
        name="projected",
    )(received, queries, unseen, chosen, w_out)
    received = lax.all_to_all(copies, "tp", 0, 0, tiled=True)
    return pl.pallas_call(
        summed_kernel,
        out_shape=jax.ShapeDtypeStruct((ROUNDS, KINDS, BATCH * R, w_out.shape[1]), bf16),
        in_specs=in_vmem(2),
        out_specs=pl.BlockSpec(memory_space=pltpu.VMEM),
        compiler_params=params,
        name="summed",
    )(received, gather)


def solution(mesh):
    in_specs = (
        P(None, None, "seq"),
        P("seq", "tp", None),
        P("tp", "seq"),
        P(None, None, "tp", None, None),
        P(None, None, "tp", None, None),
        P(None, "tp", "seq", None),
        P(None, "tp", "seq", None),
        P(None, "tp", "seq", None),
        P(None, "tp", "seq", None),
        P(None, "tp", "seq"),
        P(None, "tp", "seq"),
        P(),
        P(),
    )
    return jax.shard_map(
        per_device,
        mesh=mesh,
        in_specs=in_specs,
        out_specs=P(None, None, None, "seq"),
        check_vma=False,
    )
```

```python
import math

import jax
import jax.numpy as jnp
from jax import lax
from jax.experimental import pallas as pl
from jax.experimental.pallas import tpu as pltpu
from jax.sharding import PartitionSpec as P

HD = 128
GROUP = 8
R = 4
ROUNDS = 3
BATCH = 4
KINDS = 2
NEG = -1e30
SCALE = 1.0 / math.sqrt(HD)
SCALE_2 = SCALE / math.log(2.0)
ROWS = ROUNDS * GROUP * R
SHARE = KINDS * ROUNDS * R
NEW = ROUNDS * R
TOKENS = KINDS * ROUNDS * BATCH * R
TAIL = SHARE
PIECE = 3
MESSAGE = SHARE + 8
CHOSEN = (BATCH * 2 * 16, GROUP * BATCH * 8)
STEP = 512
FEW = 128
VMEM_LIMIT = 48 * 1024 * 1024

f32 = jnp.float32
bf16 = jnp.bfloat16


def rounded(x):
    return x.astype(bf16).astype(f32)


def dot(a, b):
    return jnp.dot(a, b, preferred_element_type=f32)


def dot_rows(a, b):
    return lax.dot_general(a, b, (((1,), (1,)), ((), ())), preferred_element_type=f32)


def parted(x):
    high = rounded(x)
    middle = rounded(x - high)
    return high, middle, x - high - middle


def by_head():
    row = lax.broadcasted_iota(jnp.int32, (KINDS * ROWS, KINDS * ROWS), 0)
    column = lax.broadcasted_iota(jnp.int32, (KINDS * ROWS, KINDS * ROWS), 1)
    target = ((column >> 2) & 7) * SHARE + ((column >> 5) << 2) + (column & 3)
    return jnp.where(row == target, 1.0, 0.0).astype(bf16)


def fresh_selection():
    row = lax.broadcasted_iota(jnp.int32, CHOSEN, 0)
    column = lax.broadcasted_iota(jnp.int32, CHOSEN, 1)
    within = (column & 7) - 1
    source = (column >> 3) * PIECE + within
    kv = jnp.where(source >= TOKENS // KINDS, 1, 0)
    token = source - kv * (TOKENS // KINDS)
    target = ((token >> 2) & 3) * 32 + kv * 16 + ((token >> 4) << 2) + (token & 3)
    taken = (within >= 0) & (within < PIECE) & (row == target)
    return jnp.where(taken, 1.0, 0.0).astype(bf16)


def token_order():
    row = lax.broadcasted_iota(jnp.int32, (TOKENS, TOKENS), 0)
    column = lax.broadcasted_iota(jnp.int32, (TOKENS, TOKENS), 1)
    at = row >> 2
    t, kind, b = at >> 3, (at >> 2) & 1, at & 3
    source = (b * KINDS * ROUNDS + kind * ROUNDS + t) * R + (row & 3)
    return jnp.where(column == source, 1.0, 0.0).astype(bf16)


def stats_spread(maxima, totals, place):
    lane = lax.broadcasted_iota(jnp.int32, (1, 128), 1)
    part = sum(jnp.where(lane >= k * SHARE, 1, 0) for k in range(1, 5))
    spread = jnp.zeros((maxima.shape[0], 128), f32)
    for k, x in enumerate(parted(maxima) + parted(totals)[:2]):
        spread = jnp.where(part == k, x, spread)
    return jnp.where(lane - part * SHARE == place, spread, 0.0)


def stats_of(rows):
    turned = rows.T
    parts = [turned[k * SHARE : (k + 1) * SHARE] for k in range(5)]
    return parts[0] + (parts[1] + parts[2]), parts[3] + parts[4]


def tails_of(received):
    return received[:, TAIL - 8 :].astype(f32)[:, 8:]


def lanes_folded(x, op):
    folded = x[:, :128]
    for k in range(1, x.shape[1] // 128):
        folded = op(folded, x[:, k * 128 : (k + 1) * 128])
    return folded


def attend(queries, keys, values, usable, scores, positions):
    step = min(STEP, positions)
    steps = range(0, positions, step)
    highest = None
    for at in steps:
        part = dot_rows(queries, keys(at, step))
        if usable is not None:
            lane = lax.broadcasted_iota(jnp.int32, (1, step), 1) + at
            part = part + jnp.where(lane < usable, 0.0, NEG)
        scores[:, at : at + step] = part
        folded = lanes_folded(part, jnp.maximum)
        highest = folded if highest is None else jnp.maximum(highest, folded)
    highest = jnp.max(highest, axis=1, keepdims=True)
    total = jnp.zeros((queries.shape[0], 128), f32)
    weighted = jnp.zeros((queries.shape[0], KINDS * HD), f32)
    for at in steps:
        weights = jnp.exp2((scores[:, at : at + step] - highest) * SCALE_2).astype(bf16)
        total = total + lanes_folded(weights.astype(f32), jnp.add)
        weighted = weighted + dot(weights, values(at, step))
    return highest * SCALE, jnp.sum(total, axis=1, keepdims=True), weighted


def partials_kernel(
    lengths_hbm,
    accepted_hbm,
    hidden_hbm,
    w_kv_hbm,
    queries_draft_hbm,
    queries_verify_hbm,
    keys_hbm,
    values_hbm,
    key_levels_hbm,
    value_levels_hbm,
    key_scales_hbm,
    value_scales_hbm,
    message,
    by_head_queries,
    unseen,
    chosen,
    gather,
    lengths,
    accepted,
    hidden,
    w_kv,
    queries_draft,
    queries_verify,
    keys,
    values,
    key_levels,
    value_levels,
    key_scales,
    value_scales,
    scores,
    order,
    tails,
    small_sems,
    cache_sems,
):
    local_len = keys.shape[1]
    few = min(FEW, local_len)
    small = [
        pltpu.make_async_copy(source, target, small_sems.at[k])
        for k, (source, target) in enumerate(
            (
                (lengths_hbm, lengths),
                (accepted_hbm, accepted),
                (queries_draft_hbm, queries_draft),
                (queries_verify_hbm, queries_verify),
                (key_scales_hbm, key_scales),
                (value_scales_hbm, value_scales),
                (hidden_hbm, hidden),
                (w_kv_hbm, w_kv),
            )
        )
    ]
    for copy in small:
        copy.start()
    order[...] = by_head()
    chosen[...] = fresh_selection()
    gather[...] = token_order()
    small[0].wait()
    first = lax.axis_index("seq") * local_len

    def usable_of(b):
        return jnp.clip(lengths[b] - first, 0, local_len)

    def cache_copies(b, rows):
        at = pl.ds(0, rows)
        return [
            pltpu.make_async_copy(source.at[b, 0, at], target.at[b, at], cache_sems.at[b, k])
            for k, (source, target) in enumerate(
                (
                    (key_levels_hbm, key_levels),
                    (keys_hbm, keys),
                    (value_levels_hbm, value_levels),
                    (values_hbm, values),
                )
            )
        ]

    for b in range(BATCH):
        usable = usable_of(b)

        @pl.when(usable > few)
        def _():
            for copy in cache_copies(b, local_len):
                copy.start()

        @pl.when((usable > 0) & (usable <= few))
        def _():
            for copy in cache_copies(b, few):
                copy.start()

    for copy in small[1:]:
        copy.wait()
    part = dot(hidden[...].reshape(ROUNDS * BATCH * R, hidden.shape[2]), w_kv[...])
    part = jnp.concatenate([part[:, :HD], part[:, HD:]], axis=0)
    row = lax.broadcasted_iota(jnp.int32, (GROUP * BATCH * 8, 2 * TOKENS // KINDS), 0)
    column = lax.broadcasted_iota(jnp.int32, (GROUP * BATCH * 8, 2 * TOKENS // KINDS), 1)
    source = (row >> 3) * PIECE + (row & 7) - 1
    high = part.astype(bf16)
    low = (part - high.astype(f32)).astype(bf16)
    to_high = ((row & 7) >= 1) & ((row & 7) <= PIECE) & (column == source)
    to_low = ((row & 7) > PIECE) & ((row & 7) <= 2 * PIECE) & (column == source - PIECE)
    tails[...] = (
        dot(jnp.where(to_high, 1.0, 0.0).astype(bf16), high)
        + dot(jnp.where(to_low, 1.0, 0.0).astype(bf16), low)
    ).reshape(tails.shape)

    row = lax.broadcasted_iota(jnp.int32, (KINDS * ROWS, 1), 0)
    place = ((row >> 5) << 2) + (row & 3)
    row = lax.broadcasted_iota(jnp.int32, (GROUP, KINDS * ROWS), 0)
    column = lax.broadcasted_iota(jnp.int32, (GROUP, KINDS * ROWS), 1)
    of_head = jnp.where(((column >> 2) & 7) == row, 1.0, 0.0).astype(bf16)
    first_row = lax.broadcasted_iota(jnp.int32, (GROUP, 8, 128), 1) == 0

    row = lax.broadcasted_iota(jnp.int32, (KINDS * ROWS, 16), 0)
    column = lax.broadcasted_iota(jnp.int32, (KINDS * ROWS, 16), 1)
    turn = (row - ((row * 171) >> 12) * SHARE) >> 2
    turn = jnp.where(turn >= ROUNDS, turn - ROUNDS, turn)
    written, token = column >> 2, column & 3
    itself = (written == turn) & (token <= (row & 3))
    earlier = written < turn
    none = jnp.where(lax.broadcasted_iota(jnp.int32, (GROUP, 8, 128), 2) < SHARE, NEG, 0.0)
    for b in range(BATCH):
        groups = [q[t, b, 0] for q in (queries_draft, queries_verify) for t in range(ROUNDS)]
        by_head_queries[b] = dot(order[...], jnp.concatenate(groups, axis=0)).astype(bf16)
        kept = jnp.where(written == 0, accepted[0, b], jnp.where(written == 1, accepted[1, b], 0))
        unseen[b] = jnp.where(itself | (earlier & (token < kept)), 0.0, NEG)
        tail = jnp.where(first_row, none, tails[:, b])
        message[:, b] = jnp.concatenate([jnp.zeros((GROUP, SHARE, HD), f32), tail], axis=1).astype(bf16)

    def sequence(b, _):
        usable = usable_of(b)

        def over(positions, masked):
            copies = cache_copies(b, positions)

            def both(levels, scales, plain, ready):
                columns = scales[b].T

                def rows(at, step):
                    if at == 0:
                        for copy in ready:
                            copy.wait()
                    low = [
                        (levels[b, k : k + 128].astype(f32) * columns[:, k // 128 : k // 128 + 1]).astype(bf16)
                        for k in range(at, at + step, 128)
                    ]
                    return jnp.concatenate([jnp.concatenate(low, axis=0), plain[b, at : at + step]], axis=1)

                return rows

            zeros = jnp.zeros((ROWS, HD), bf16)
            rows = jnp.concatenate(
                [
                    jnp.concatenate([queries_draft[:, b, 0].reshape(ROWS, HD), zeros], axis=1),
                    jnp.concatenate([zeros, queries_verify[:, b, 0].reshape(ROWS, HD)], axis=1),
                ],
                axis=0,
            )
            maxima, totals, weighted = attend(
                rows,
                both(key_levels, key_scales, keys, copies[:2]),
                both(value_levels, value_scales, values, copies[2:]),
                usable if masked else None,
                scores,
                positions,
            )
            sums = jnp.concatenate([weighted[:ROWS, :HD], weighted[ROWS:, HD:]], axis=0).astype(bf16)
            stats = stats_spread(maxima, totals, place).astype(bf16)
            ordered = dot(order[...], sums).reshape(GROUP, SHARE, HD)
            tail = jnp.where(first_row, dot(of_head, stats).reshape(GROUP, 1, 128), tails[:, b])
            message[:, b] = jnp.concatenate([ordered, tail], axis=1).astype(bf16)

        @pl.when((usable > 0) & (usable <= few))
        def _():
            over(few, True)

        @pl.when((usable > few) & (usable < local_len))
        def _():
            over(local_len, True)

        @pl.when(usable == local_len)
        def _():
            over(local_len, False)

        return 0

    lax.fori_loop(0, BATCH, sequence, 0)


def partials(lengths, accepted, *arrays):
    local_len = arrays[4].shape[2]
    hidden, w_kv, queries = arrays[:3]
    blocks = local_len // 128
    return pl.pallas_call(
        partials_kernel,
        out_shape=[
            jax.ShapeDtypeStruct((GROUP, BATCH, MESSAGE, HD), bf16),
            jax.ShapeDtypeStruct((BATCH, KINDS * ROWS, HD), bf16),
            jax.ShapeDtypeStruct((BATCH, KINDS * ROWS, 16), f32),
            jax.ShapeDtypeStruct(CHOSEN, bf16),
            jax.ShapeDtypeStruct((TOKENS, TOKENS), bf16),
        ],
        in_specs=[pl.BlockSpec(memory_space=pltpu.HBM)] * (2 + len(arrays)),
        out_specs=[pl.BlockSpec(memory_space=pltpu.VMEM)] * 5,
        scratch_shapes=[
            pltpu.SMEM((BATCH,), jnp.int32),
            pltpu.SMEM(accepted.shape, jnp.int32),
            pltpu.VMEM(hidden.shape, bf16),
            pltpu.VMEM(w_kv.shape, bf16),
            pltpu.VMEM(queries.shape, bf16),
            pltpu.VMEM(queries.shape, bf16),
            pltpu.VMEM((BATCH, local_len, HD), bf16),
            pltpu.VMEM((BATCH, local_len, HD), bf16),
            pltpu.VMEM((BATCH, local_len, HD), bf16),
            pltpu.VMEM((BATCH, local_len, HD), bf16),
            pltpu.VMEM((BATCH, blocks, 128), f32),
            pltpu.VMEM((BATCH, blocks, 128), f32),
            pltpu.VMEM((KINDS * ROWS, local_len), f32),
            pltpu.VMEM((KINDS * ROWS, KINDS * ROWS), bf16),
            pltpu.VMEM((GROUP, BATCH, 8, 128), f32),
            pltpu.SemaphoreType.DMA((8,)),
            pltpu.SemaphoreType.DMA((BATCH, 4)),
        ],
        compiler_params=pltpu.CompilerParams(vmem_limit_bytes=VMEM_LIMIT),
        name="partials",
    )(*(pltpu.with_memory_space_constraint(x, pltpu.HBM) for x in (lengths, accepted, *arrays)))


def joined_kernel(received, copies):
    peers = received.shape[0]
    tails = tails_of(received)
    maxima, totals = stats_of(tails[:, 0])
    highest = jnp.max(maxima, axis=1, keepdims=True)
    factors = jnp.exp(maxima - highest)
    total = jnp.sum(totals * factors, axis=1, keepdims=True)
    chains = [jnp.zeros((SHARE, HD), f32)] * 4
    for s in range(peers):
        chains[s % 4] += factors[:, s : s + 1] * received[s].astype(f32)[:SHARE]
    sums = (chains[0] + chains[1]) + (chains[2] + chains[3])
    fresh = jnp.sum(tails, axis=0)
    fresh = fresh + jnp.concatenate([fresh[PIECE:], fresh[:PIECE]], axis=0)
    place = lax.broadcasted_iota(jnp.int32, (SHARE, 1), 0)
    stats = jnp.sum(stats_spread(highest, total, place), axis=0, keepdims=True)
    row = lax.broadcasted_iota(jnp.int32, (8, 128), 0)
    tail = jnp.where(row == 0, stats, jnp.where(row <= PIECE, fresh, 0.0))
    block = jnp.concatenate([sums / total, tail], axis=0).astype(bf16)
    for s in range(peers):
        copies[s] = block


def projected_kernel(received, queries, unseen, chosen, w_out, copies):
    peers = received.shape[0]
    tails = tails_of(received)
    fresh = dot(chosen[...], tails.reshape(peers * 8, 128).astype(bf16)).astype(bf16)
    maxima, totals = stats_of(tails[:, 0])
    parts = []
    for b in range(BATCH):
        scores = dot_rows(queries[b], fresh[b * 32 : b * 32 + 16]) * SCALE
        scores = jnp.where(unseen[b] == 0.0, scores, NEG)
        new_highest = jnp.max(scores, axis=1, keepdims=True)
        weights = jnp.exp(scores - new_highest).astype(bf16)
        new_total = jnp.sum(weights.astype(f32), axis=1, keepdims=True)
        new_sums = dot(weights, fresh[b * 32 + 16 : b * 32 + 32])
        of_b = range(b, peers, BATCH)
        highest = jnp.concatenate([maxima[:, p : p + 1] for p in of_b], axis=0)
        total = jnp.concatenate([totals[:, p : p + 1] for p in of_b], axis=0)
        means = jnp.concatenate([received[p].astype(f32)[:SHARE] for p in of_b], axis=0)
        overall = jnp.maximum(highest, new_highest)
        factor = total * jnp.exp(highest - overall)
        new_factor = jnp.exp(new_highest - overall)
        whole = factor + new_total * new_factor
        attended = means * (factor / whole) + new_sums * (new_factor / whole)
        parts.append(
            jnp.concatenate([attended[g * SHARE : (g + 1) * SHARE] for g in range(GROUP)], axis=1)
        )
    out = dot(jnp.concatenate(parts, axis=0).astype(bf16), w_out[...]).astype(bf16)
    for k in range(copies.shape[0]):
        copies[k] = out


def summed_kernel(received, gather, out):
    total = received[0].astype(f32)
    for k in range(1, received.shape[0]):
        total = total + received[k].astype(f32)
    ordered = dot(gather[...], total.astype(bf16)).astype(bf16)
    out[...] = ordered.reshape(out.shape)


def in_vmem(count):
    return [pl.BlockSpec(memory_space=pltpu.VMEM)] * count


def per_device(
    hidden_new,
    w_kv,
    w_out,
    queries_draft,
    queries_verify,
    keys_cache,
    values_cache,
    key_levels,
    value_levels,
    key_scales,
    value_scales,
    lengths,
    accepted,
):
    peers, heads = lax.axis_size("seq"), lax.axis_size("tp")
    params = pltpu.CompilerParams(vmem_limit_bytes=VMEM_LIMIT)
    scales = [x.reshape(BATCH, -1, 128) for x in (key_scales, value_scales)]
    message, queries, unseen, chosen, gather = partials(
        lengths,
        accepted,
        hidden_new,
        w_kv.reshape(w_kv.shape[0], -1),
        queries_draft,
        queries_verify,
        keys_cache,
        values_cache,
        key_levels,
        value_levels,
        *scales,
    )
    received = lax.all_to_all(message.reshape(peers, MESSAGE, HD), "seq", 0, 0, tiled=True)
    copies = pl.pallas_call(
        joined_kernel,
        out_shape=jax.ShapeDtypeStruct((peers, MESSAGE, HD), bf16),
        in_specs=in_vmem(1),
        out_specs=pl.BlockSpec(memory_space=pltpu.VMEM),
        compiler_params=params,
        name="joined",
    )(received)
    received = lax.all_to_all(copies, "seq", 0, 0, tiled=True)
    copies = pl.pallas_call(
        projected_kernel,
        out_shape=jax.ShapeDtypeStruct((heads, TOKENS, w_out.shape[1]), bf16),
        in_specs=in_vmem(5),
        out_specs=pl.BlockSpec(memory_space=pltpu.VMEM),
        compiler_params=params,
        name="projected",
    )(received, queries, unseen, chosen, w_out)
    received = lax.all_to_all(copies, "tp", 0, 0, tiled=True)
    return pl.pallas_call(
        summed_kernel,
        out_shape=jax.ShapeDtypeStruct((ROUNDS, KINDS, BATCH * R, w_out.shape[1]), bf16),
        in_specs=in_vmem(2),
        out_specs=pl.BlockSpec(memory_space=pltpu.VMEM),
        compiler_params=params,
        name="summed",
    )(received, gather)


def solution(mesh):
    in_specs = (
        P(None, None, "seq"),
        P("seq", "tp", None),
        P("tp", "seq"),
        P(None, None, "tp", None, None),
        P(None, None, "tp", None, None),
        P(None, "tp", "seq", None),
        P(None, "tp", "seq", None),
        P(None, "tp", "seq", None),
        P(None, "tp", "seq", None),
        P(None, "tp", "seq"),
        P(None, "tp", "seq"),
        P(),
        P(),
    )
    return jax.shard_map(
        per_device,
        mesh=mesh,
        in_specs=in_specs,
        out_specs=P(None, None, None, "seq"),
        check_vma=False,
    )
```
